32 devices in a mesh: segment: 4 (over y, x), expert: 4 (over z), dp: 2 (over core).
Axes of the slice: x: 2, y: 2, z: 4, core: 2. Of those that a mesh axis runs over, the one named last changes fastest.
Arguments:
- activations: bfloat16 [4, 256, 8, 512], P('segment', ('expert', 'dp')), may hold values from -6 to 6
- upstream: bfloat16 [4, 256, 8, 512], P('segment', ('expert', 'dp')), may hold values from -6 to 6
- routes: int32 [4, 256, 2], P('segment', ('expert', 'dp')), may hold values from 0 to 3, all different within a row; in each aligned block of 32 rows (0 to 31, 32 to 63, ..., all dimensions but the last counted through in order) at most 32 rows name the same one
- gate_codes: int32 [4, 256, 2], P('segment', ('expert', 'dp')), may hold values from 1 to 32767
- weights: bfloat16 [4, 4, 9, 64, 512], P('segment', 'expert'), may hold values from -0.25 to 0.25
Outputs:
- input_grad: bfloat16 [4, 256, 8, 512], P('segment', ('expert', 'dp'))
- weight_grad: float32 [4, 4, 9, 64, 512], P('segment', 'expert')
The draws below stay inside these ranges and needn't reach their ends.
Inputs may be any that keep to these rules, and one draw needn't show every extreme that they name: `routes`: the two experts of a tile differ; the 32 tiles of one device name each expert at most 32 times, and on some devices one expert exactly 32 times.
All inputs are finite; a program needn't handle non-finite values.
Results may differ from the reference program's by a relative error of at most 0.004.
Values may be sent and summed in bfloat16 or wider, within the bound.
No kernel may reach another device: no remote copies, remote signals or barrier semaphores. Data moves between devices by JAX's collectives and lax.ppermute only.
A program may use at most 64 MiB of HBM per device.

```python
import math
import jax
import jax.numpy as jnp
import numpy as np
from jax import lax

C = 512
GW = 64
TH = 4
TW = 2
CELLS = 8
TPD = 32
EXPERTS = 4
CAP = 32
SEGMENTS = 4
TILES = 256
N_EXPERT = 4
N_DP = 2


def touch_ends(array, own_key, smallest, top_value):
    longest = array.shape.index(max(array.shape))
    spots = []
    for shift in (0, 1):
        where = [jax.random.randint(jax.random.fold_in(own_key, axis), (), 0, length) for axis, length in enumerate(array.shape)]
        where[longest] = (where[longest] + shift) % array.shape[longest]
        spots.append(tuple(where))
    return array.at[spots[0]].set(smallest).at[spots[1]].set(top_value)


def level_of(key, dims, split, least, top_value):
    level = 1.0
    for axis_at, parts in split:
        draws = jax.random.uniform(jax.random.fold_in(jax.random.fold_in(key, 6), axis_at), (parts,), jnp.float32, least / len(split), top_value / len(split))
        level = level * jnp.repeat(jnp.exp(draws), dims[axis_at] // parts).reshape((-1,) + (1,) * (len(dims) - 1 - axis_at))
    return level


def deal_out(rng, own, number, rows, amount, top, reach, slope):
    order = jax.random.permutation(rng, amount)
    packed, ordinary = portions_of(amount, rows * top, reach, slope, True), portions_of(amount, rows * top, reach, slope, False)
    places = jnp.arange(amount)

    def named(lengths, rotation):
        used = int((lengths > 0).sum())
        fixed = max(1, used // 4)
        passed = fixed + (places - fixed + rotation * (used - fixed)) % max(1, amount - fixed)
        return jnp.zeros((amount,), jnp.int32).at[order[jnp.where(places < fixed, places, passed)]].set(jnp.asarray(lengths, jnp.int32))

    lengths = jnp.where(number % 4 == 0, named(packed, number // 4), named(ordinary, number - number // 4 - 1))
    mixed = jax.random.permutation(jax.random.fold_in(own, 3), amount)
    giver, receiver = mixed[0:amount // 2 * 2:2], mixed[1:amount // 2 * 2:2]
    room = jnp.minimum(lengths[giver] - 1, reach - lengths[receiver]) // 2
    room = jnp.where((giver == order[0]) | (receiver == order[0]) | (lengths[receiver] == 0), 0, jnp.maximum(room, 0))
    passed = jax.random.randint(jax.random.fold_in(own, 4), (amount // 2,), 0, 1 << 20) % (room + 1)
    lengths = lengths.at[giver].add(-passed).at[receiver].add(passed)
    items = jnp.searchsorted(jnp.cumsum(lengths), jnp.arange(rows * top), side="right").astype(jnp.int32)
    listing = items.reshape(top, rows).T
    listing = listing[jax.random.permutation(jax.random.fold_in(own, 1), rows)]
    rotation = jax.random.randint(jax.random.fold_in(own, 2), (rows, 1), 0, top)
    return jnp.take_along_axis(listing, (jnp.arange(top)[None, :] + rotation) % top, axis=1)


def portions_of(count, total, limit, lean, full):
    loads = [(1 << 20) // math.isqrt(rank ** lean) + 1 for rank in range(1, count + 1)]
    largest = limit if full else min(limit, max(-(-total // count), total * loads[0] // sum(loads)))
    least = 1 if total - largest >= count - 1 else 0
    counts, surplus = [largest] + [least] * (count - 1), total - largest - least * (count - 1)
    while surplus > 0:
        candidates = [i for i in range(1, count) if counts[i] < largest] or [i for i in range(1, count) if counts[i] < limit]
        pool, budget = sum([loads[i] for i in candidates]), surplus
        for i in candidates:
            extra = min(limit - counts[i], max(1, budget * loads[i] // pool), surplus)
            counts[i] = counts[i] + extra
            surplus = surplus - extra
    return np.array(counts)


def centred(rng, shape, width, bound, shards=(), kind=jnp.bfloat16):
    entries = width * jax.random.normal(rng, shape, jnp.float32)
    if shards:
        entries = entries * level_of(rng, shape, shards, -0.22, 0.18)
    return jnp.clip(entries, -bound, bound).astype(kind)


def setup_inputs(seed: int = 0) -> dict:
    splits = jax.random.split(jax.random.key(seed), 6)
    activations = centred(splits[0], (SEGMENTS, TILES, CELLS, C), 1.0, 6.0, ((0, 4), (1, 8)))
    upstream = centred(splits[1], (SEGMENTS, TILES, CELLS, C), 1.0, 6.0, ((0, 4), (1, 8)))
    routes_keys = jax.random.split(jax.random.fold_in(splits[2], 1), SEGMENTS * TILES // TPD)
    routes_turns = jax.random.permutation(jax.random.fold_in(splits[2], 3), SEGMENTS * TILES // TPD)
    routes = jax.vmap(lambda own, number: deal_out(jax.random.fold_in(splits[2], 2), own, number, TPD, EXPERTS, 2, CAP, 2))(routes_keys, routes_turns).reshape((SEGMENTS, TILES, 2))
    gate_codes = touch_ends(jax.random.randint(splits[3], (SEGMENTS, TILES, 2), 1, 32768), jax.random.fold_in(splits[3], 1), 1, 32767).astype(jnp.int32)
    weights = centred(splits[4], (SEGMENTS, EXPERTS, 9, GW, C), (9 * GW) ** -0.5, 0.25, ((0, 4), (1, 4)))
    return {"activations": activations, "upstream": upstream, "routes": routes, "gate_codes": gate_codes, "weights": weights}


def transpose_conv(scaled_grads, weight):
    tile_count = scaled_grads.shape[0]
    group_width = weight.shape[1]
    channels = weight.shape[2]
    group_count = channels // group_width
    padded = jnp.pad(scaled_grads.reshape(tile_count, TH, TW, channels), ((0, 0), (1, 1), (1, 1), (0, 0)))
    summed = jnp.zeros((tile_count, TH, TW, group_count, group_width), jnp.float32)
    for row_off in (-1, 0, 1):
        for col_off in (-1, 0, 1):
            tap_index = (row_off + 1) * 3 + (col_off + 1)
            shifted = padded[:, 1 - row_off:1 - row_off + TH, 1 - col_off:1 - col_off + TW, :]
            shifted = shifted.reshape(tile_count, TH, TW, group_count, group_width).astype(jnp.float32)
            kernel = weight[tap_index].reshape(group_width, group_count, group_width).astype(jnp.float32)
            summed = summed + jnp.einsum('nijgo,cgo->nijgc', shifted, kernel)
    return summed.reshape(tile_count, TH * TW, channels)


def weight_corr(inputs, scaled_grads, group_width):
    tile_count = inputs.shape[0]
    channels = inputs.shape[2]
    group_count = channels // group_width
    padded = jnp.pad(inputs.reshape(tile_count, TH, TW, channels), ((0, 0), (1, 1), (1, 1), (0, 0)))
    grads = scaled_grads.reshape(tile_count, TH, TW, group_count, group_width).astype(jnp.float32)
    taps = []
    for row_off in (-1, 0, 1):
        for col_off in (-1, 0, 1):
            shifted = padded[:, 1 + row_off:1 + row_off + TH, 1 + col_off:1 + col_off + TW, :]
            shifted = shifted.reshape(tile_count, TH, TW, group_count, group_width).astype(jnp.float32)
            taps.append(jnp.einsum('nijgc,nijgo->cgo', shifted, grads).reshape(group_width, channels))
    return jnp.stack(taps, axis=0)


def reference(activations, upstream, routes, gate_codes, weights):
    route_total = 2 * TILES
    slot_limit = CAP * N_EXPERT * N_DP

    def one_segment(segment_index):
        incoming = lax.dynamic_index_in_dim(upstream, (segment_index + 1) % SEGMENTS, 0, keepdims=False)
        inputs = lax.dynamic_index_in_dim(activations, segment_index, 0, keepdims=False)
        route_ids = lax.dynamic_index_in_dim(routes, segment_index, 0, keepdims=False)
        code_values = lax.dynamic_index_in_dim(gate_codes, segment_index, 0, keepdims=False).astype(jnp.float32)
        segment_weights = lax.dynamic_index_in_dim(weights, segment_index, 0, keepdims=False)
        gate_share = code_values / jnp.sum(code_values, axis=1, keepdims=True)
        scaled_grads = (gate_share[:, :, None, None] * incoming[:, None].astype(jnp.float32)).astype(jnp.bfloat16)
        flat_expert = route_ids.reshape(-1)
        matches = (flat_expert[:, None] == jnp.arange(EXPERTS, dtype=jnp.int32)[None, :]).astype(jnp.int32)
        earlier = jnp.cumsum(matches, axis=0) - matches
        slot_rank = jnp.sum(earlier * matches, axis=1).astype(jnp.int32)
        route_table = jnp.full((EXPERTS, slot_limit), route_total, jnp.int32)
        route_table = route_table.at[flat_expert, slot_rank].set(jnp.arange(route_total, dtype=jnp.int32))
        empty_row = jnp.zeros((1, TH * TW, C), jnp.bfloat16)
        grad_rows = jnp.concatenate([scaled_grads.reshape(route_total, TH * TW, C), empty_row], axis=0)
        input_rows = jnp.concatenate([jnp.repeat(inputs, 2, axis=0), empty_row], axis=0)

        def per_expert(expert_index):
            chosen = route_table[expert_index]
            grads_here = grad_rows[chosen]
            inputs_here = input_rows[chosen]
            kernel = lax.dynamic_index_in_dim(segment_weights, expert_index, 0, keepdims=False)
            answers = transpose_conv(grads_here, kernel).astype(jnp.bfloat16)
            return answers, weight_corr(inputs_here, grads_here, GW)

        answers, kernel_grads = lax.map(per_expert, jnp.arange(EXPERTS, dtype=jnp.int32))
        per_route = answers[flat_expert, slot_rank].astype(jnp.float32).reshape(TILES, 2, TH * TW, C)
        input_grad = (incoming.astype(jnp.float32) + per_route[:, 0] + per_route[:, 1]).astype(jnp.bfloat16)
        return input_grad, kernel_grads / TPD

    input_grad, weight_grad = lax.map(one_segment, jnp.arange(SEGMENTS, dtype=jnp.int32))
    return input_grad, weight_grad
```

```python
import jax
import jax.numpy as jnp
import numpy as np
from jax import lax
from jax.experimental import pallas as pl
from jax.experimental.pallas import tpu as pltpu
from jax.sharding import PartitionSpec as P

TH = 4
TW = 2


def shifted(array, axis, by):
    count = lax.axis_size(axis)
    return lax.ppermute(array, axis, [(i, (i + by) % count) for i in range(count)])


def offsets_table():
    cell_count = TH * TW
    table = np.zeros((cell_count, cell_count, 9), np.float32)
    for source_cell in range(cell_count):
        for target_cell in range(cell_count):
            row_step = target_cell // TW - source_cell // TW
            col_step = target_cell % TW - source_cell % TW
            if abs(row_step) <= 1 and abs(col_step) <= 1:
                table[source_cell, target_cell, (row_step + 1) * 3 + col_step + 1] = 1.0
    return table


def by_group(rows, group_width):
    tile_count = rows.shape[0]
    cell_count = rows.shape[1]
    group_count = rows.shape[2] // group_width
    split = rows.reshape(tile_count, cell_count, group_count, group_width).transpose(2, 0, 1, 3)
    return split.reshape(group_count, tile_count, cell_count * group_width)


def transpose_conv(scaled_grads, weight):
    tile_count = scaled_grads.shape[0]
    cell_count = scaled_grads.shape[1]
    group_width = weight.shape[1]
    channels = weight.shape[2]
    group_count = channels // group_width
    selector = jnp.asarray(offsets_table(), jnp.bfloat16)
    split_weight = weight.reshape(9, group_width, group_count, group_width)
    blocks = jnp.einsum(
        "pqt,tcgo->gpoqc", selector, split_weight, preferred_element_type=jnp.float32
    )
    blocks = blocks.astype(jnp.bfloat16).reshape(
        group_count, cell_count * group_width, cell_count * group_width
    )
    grouped = by_group(scaled_grads, group_width)
    result = jnp.einsum("gnk,gkm->gnm", grouped, blocks, preferred_element_type=jnp.float32)
    result = result.reshape(group_count, tile_count, cell_count, group_width).transpose(1, 2, 0, 3)
    return result.reshape(tile_count, cell_count, channels)


def weight_corr(inputs, scaled_grads, group_width):
    cell_count = inputs.shape[1]
    channels = inputs.shape[2]
    group_count = channels // group_width
    grouped_inputs = by_group(inputs, group_width)
    grouped_grads = by_group(scaled_grads, group_width)
    moments = jnp.einsum(
        "gnk,gnm->gkm", grouped_inputs, grouped_grads, preferred_element_type=jnp.float32
    )
    moments = moments.reshape(group_count, cell_count, group_width, cell_count, group_width)
    selector = jnp.asarray(offsets_table(), jnp.float32)
    taps = jnp.einsum("gpcqo,qpt->tcgo", moments, selector, precision=lax.Precision.HIGHEST)
    return taps.reshape(9, group_width, channels)


def body(activations, upstream, routes, gate_codes, weights):
    incoming = shifted(upstream, "segment", -1)[0]
    inputs = activations[0]
    route_ids = routes[0]
    code_values = gate_codes[0].astype(jnp.float32)
    kernel = weights[0, 0]
    group_width = kernel.shape[1]
    per_device = inputs.shape[0]
    cell_count = inputs.shape[1]
    channels = inputs.shape[2]
    experts = lax.axis_size("expert")
    capacity = max(2, 4 * per_device // experts)
    gate_share = code_values / jnp.sum(code_values, axis=1, keepdims=True)
    scaled_grads = (gate_share[:, :, None, None] * incoming[:, None].astype(jnp.float32)).astype(
        jnp.bfloat16
    )
    grad_rows = scaled_grads.reshape(2 * per_device, cell_count * channels)
    input_rows = jnp.repeat(inputs, 2, axis=0).reshape(2 * per_device, cell_count * channels)
    flat_expert = route_ids.reshape(-1)
    matches = (flat_expert[:, None] == jnp.arange(experts, dtype=jnp.int32)[None, :]).astype(
        jnp.int32
    )
    earlier = jnp.cumsum(matches, axis=0) - matches
    slot_rank = jnp.sum(earlier * matches, axis=1)
    slot_place = flat_expert * capacity + slot_rank
    chooser = (
        slot_place[None, :] == jnp.arange(experts * capacity, dtype=jnp.int32)[:, None]
    ).astype(jnp.bfloat16)

    def pack_slots(rows):
        packed = jnp.dot(chooser, rows, preferred_element_type=jnp.float32).astype(jnp.bfloat16)
        return packed.reshape(experts, capacity, cell_count, channels)

    inputs_recv, grads_recv = (
        lax.all_to_all(pack_slots(input_rows), "expert", split_axis=0, concat_axis=0, tiled=True),
        lax.all_to_all(pack_slots(grad_rows), "expert", split_axis=0, concat_axis=0, tiled=True),
    )
    flat_grads = grads_recv.reshape(experts * capacity, cell_count, channels)
    answers = transpose_conv(flat_grads, kernel).astype(jnp.bfloat16)
    returned = lax.all_to_all(
        answers.reshape(experts, capacity, cell_count, channels),
        "expert",
        split_axis=0,
        concat_axis=0,
        tiled=True,
    )
    flat_inputs = inputs_recv.reshape(experts * capacity, cell_count, channels)
    local_grad = weight_corr(flat_inputs, flat_grads, group_width)
    flat_answers = returned.reshape(experts * capacity, cell_count * channels)
    per_route = jnp.dot(chooser.T, flat_answers, preferred_element_type=jnp.float32).reshape(
        per_device, 2, cell_count, channels
    )
    input_grad = (incoming.astype(jnp.float32) + per_route[:, 0] + per_route[:, 1]).astype(
        jnp.bfloat16
    )
    total_grad = lax.psum(local_grad, "dp") / per_device
    return (input_grad[None], total_grad[None, None])


LINE = 4
NEAR_PAIRS = [(0, 1), (1, 0), (2, 3), (3, 2)]
INNER_PAIRS = [(1, 2), (2, 1)]
SWAP = [(0, 1), (1, 0)]
VMEM_LIMIT = 56 * 1024 * 1024


def fits_line(mesh):
    return mesh.shape["expert"] == LINE and mesh.shape["dp"] == 2


def cell_order():
    return [row * TW + col for col in range(TW) for row in range(TH)]


def own_gates(info, expert):
    codes = info[2:4].astype(jnp.float32)
    hits = jnp.where(info[0:2] == expert, codes, 0.0)
    return (hits[0:1] + hits[1:2]) / (codes[0:1] + codes[1:2])


def gate_columns(info_ref, experts):
    rows = [own_gates(info_ref[...], expert) for expert in experts]
    count = rows[0].shape[1]
    table = jnp.concatenate(rows + [jnp.zeros((8 - len(rows), count), jnp.float32)], axis=0)
    table = jnp.concatenate([table, jnp.zeros((8, 128 - count), jnp.float32)], axis=1)
    return table.T[:count]


def slot_experts():
    me = lax.axis_index("expert")
    outer = (me == 0) | (me == 3)
    mid = jnp.where(outer, 2, 3)
    far = 5 - mid
    return [me, me ^ 1, me ^ mid, me ^ far]


def partial_kernel(
    grad_a, grad_b, act_a, act_b, info_a, info_b, scaled_ref, own_ref, near_ref, mid_ref, far_ref, wide, cells, turned
):
    tiles = info_a.shape[1]
    block = 2 * tiles
    width = grad_a.shape[1]
    column = TH * block
    strips = width // 128
    for at, ref in enumerate((grad_a, grad_b, act_a, act_b)):
        for strip in range(strips):
            wide[at * strips + strip] = ref[:, pl.ds(strip * 128, 128)].astype(jnp.float32)

    def cell_rows(at, cell):
        pieces = [wide[at * strips + strip, pl.ds(cell, tiles, stride=TH * TW), :] for strip in range(strips)]
        return jnp.concatenate(pieces, axis=1)

    experts = slot_experts()
    gates_a = gate_columns(info_a, experts)
    gates_b = gate_columns(info_b, experts)
    order = cell_order()
    for place, cell in enumerate(order):
        part_a = cell_rows(0, cell)
        part_b = cell_rows(1, cell)
        for slot in range(4):
            both = jnp.concatenate(
                [part_a * gates_a[:, slot : slot + 1], part_b * gates_b[:, slot : slot + 1]], axis=0
            )
            scaled_ref[slot, pl.ds(place * block, block), :] = both.astype(jnp.bfloat16)
        act_rows = jnp.concatenate([cell_rows(2, cell), cell_rows(3, cell)], axis=0)
        cells[pl.ds(place * block, block), :] = act_rows.astype(jnp.bfloat16)
    empty = jnp.zeros((block, width), jnp.bfloat16)
    for col in range(TW):
        rows = cells[pl.ds(col * column, column), :]
        turned[1, :, pl.ds(col * column, column)] = rows.T
        turned[2, :, pl.ds(col * column, column)] = jnp.concatenate([rows[block:], empty], axis=0).T
        turned[0, :, pl.ds(col * column, column)] = jnp.concatenate([empty, rows[:-block]], axis=0).T
    low_half = lax.broadcasted_iota(jnp.int32, (64, 128), 1) < 64
    for slot, ref in ((3, far_ref), (2, mid_ref), (1, near_ref), (0, own_ref)):
        for row_off in (-1, 0, 1):
            for col_off in (-1, 0, 1):
                lhs = turned[row_off + 1]
                rhs = scaled_ref[slot]
                if col_off == 1:
                    lhs, rhs = lhs[:, column:], rhs[:column]
                if col_off == -1:
                    lhs, rhs = lhs[:, :column], rhs[column:]
                full = jnp.dot(lhs, rhs, preferred_element_type=jnp.float32)
                tap = (row_off + 1) * 3 + col_off + 1
                for pair in range(width // 128):
                    base = pair * 128
                    piece = jnp.where(
                        low_half,
                        full[base : base + 64, base : base + 128],
                        full[base + 64 : base + 128, base : base + 128],
                    )
                    ref[tap, :, pl.ds(base, 128)] = piece.astype(ref.dtype)


def answer_kernel(scaled_ref, own_ref, near_ref, mid_ref, far_ref, grad_a, grad_b, out_a, out_b, total, spread):
    width = grad_a.shape[1]
    tiles = grad_a.shape[0] // (TH * TW)
    block = 2 * tiles
    lane_group = lax.broadcasted_iota(jnp.int32, (64, width), 1) // 64
    masks = [jnp.where(lane_group == g, 1.0, 0.0).astype(jnp.bfloat16) for g in range(width // 64)]
    total[...] = jnp.zeros_like(total)
    for slot, ref in enumerate((own_ref, near_ref, mid_ref, far_ref)):
        for row_off in (-1, 0, 1):
            for col_off in (-1, 0, 1):
                tap = (row_off + 1) * 3 + col_off + 1
                kernel = ref[tap]
                blocks = jnp.concatenate([kernel * mask for mask in masks], axis=0)
                first = max(0, -row_off)
                rows = (TH - abs(row_off)) * block
                for col in range(TW):
                    if not 0 <= col + col_off < TW:
                        continue
                    source = (col * TH + first) * block
                    target = ((col + col_off) * TH + first + row_off) * block
                    total[pl.ds(target, rows), :] += lax.dot_general(
                        scaled_ref[slot, pl.ds(source, rows), :],
                        blocks,
                        (((1,), (1,)), ((), ())),
                        preferred_element_type=jnp.float32,
                    )
    for at, (grad, out) in enumerate(((grad_a, out_a), (grad_b, out_b))):
        for place, cell in enumerate(cell_order()):
            for strip in range(width // 128):
                spread[strip, pl.ds(cell, tiles, stride=TH * TW), :] = total[
                    pl.ds(place * block + at * tiles, tiles), pl.ds(strip * 128, 128)
                ]
        for strip in range(width // 128):
            lanes = pl.ds(strip * 128, 128)
            out[:, lanes] = (grad[:, lanes].astype(jnp.float32) + spread[strip]).astype(jnp.bfloat16)


def on_vmem(count):
    return [pl.BlockSpec(memory_space=pltpu.VMEM)] * count


def weights_travel(activations, upstream, routes, gate_codes, weights):
    me = lax.axis_index("expert")
    core = lax.axis_index("dp")
    inner = (me == 1) | (me == 2)
    per_device, cell_count, channels = activations.shape[1:]
    rows = per_device * cell_count
    width = channels // 2
    kernel = weights[0, 0]
    taps, group_width = kernel.shape[0], kernel.shape[1]
    sections = lax.axis_size("segment")

    def half(array, which):
        return lax.dynamic_slice_in_dim(array, which * width, width, array.ndim - 1)

    def along(array, pairs):
        return lax.ppermute(array, "expert", pairs)

    def from_next(array, flip):
        pairs = []
        for s in range(sections):
            for d in range(2):
                pairs.append((2 * ((s + 1) % sections) + d, 2 * s + (1 - d if flip else d)))
        return lax.ppermute(array, ("segment", "dp"), pairs)

    upstream_rows = upstream[0].reshape(rows, channels)
    act_rows = activations[0].reshape(rows, channels)
    info = jnp.concatenate([routes[0].T, gate_codes[0].T], axis=0)
    my_weights = half(kernel, core)
    inner_weights = along(my_weights, INNER_PAIRS)
    near_weights = along(my_weights, NEAR_PAIRS)
    grad_a = from_next(half(upstream_rows, core), False)
    grad_b = from_next(half(upstream_rows, 1 - core), True)
    act_a = half(act_rows, core)
    act_b = lax.ppermute(half(act_rows, 1 - core), "dp", SWAP)
    info_b = lax.ppermute(info, "dp", SWAP)

    part = jax.ShapeDtypeStruct((taps, group_width, width), jnp.bfloat16)
    scaled, own_part, near_part, mid_part, far_part = pl.pallas_call(
        partial_kernel,
        out_shape=(
            jax.ShapeDtypeStruct((4, 2 * rows, width), jnp.bfloat16),
            jax.ShapeDtypeStruct((taps, group_width, width), jnp.float32),
            part,
            part,
            part,
        ),
        in_specs=on_vmem(6),
        out_specs=tuple(on_vmem(5)),
        scratch_shapes=[
            pltpu.VMEM((4 * (width // 128), rows, 128), jnp.float32),
            pltpu.VMEM((2 * rows, width), jnp.bfloat16),
            pltpu.VMEM((3, width, 2 * rows), jnp.bfloat16),
        ],
        compiler_params=pltpu.CompilerParams(vmem_limit_bytes=VMEM_LIMIT),
        cost_estimate=pl.CostEstimate(flops=3_000_000_000, bytes_accessed=3_000_000, transcendentals=0),
    )(grad_a, grad_b, act_a, act_b, info, info_b)

    cross_weights = along(near_weights, INNER_PAIRS)
    first_swap = along(jnp.where(inner, inner_weights, far_part), NEAR_PAIRS)
    second_swap = along(jnp.where(inner, cross_weights, mid_part), NEAR_PAIRS)
    far_sum = along(far_part + first_swap, INNER_PAIRS)
    mid_sum = along(mid_part + second_swap, INNER_PAIRS)
    last_swap = along(near_part + far_sum, NEAR_PAIRS)

    mid_weights = jnp.where(inner, inner_weights, first_swap)
    far_weights = jnp.where(inner, cross_weights, second_swap)
    answer = jax.ShapeDtypeStruct((rows, width), jnp.bfloat16)
    grad_own, grad_other = pl.pallas_call(
        answer_kernel,
        out_shape=(answer, answer),
        in_specs=on_vmem(7),
        out_specs=tuple(on_vmem(2)),
        scratch_shapes=[
            pltpu.VMEM((2 * rows, width), jnp.float32),
            pltpu.VMEM((width // 128, rows, 128), jnp.float32),
        ],
        compiler_params=pltpu.CompilerParams(vmem_limit_bytes=VMEM_LIMIT),
        cost_estimate=pl.CostEstimate(flops=3_000_000_000, bytes_accessed=3_000_000, transcendentals=0),
    )(scaled, my_weights, near_weights, mid_weights, far_weights, grad_a, grad_b)
    grad_back = lax.ppermute(grad_other, "dp", SWAP)

    def whole(mine, other):
        return jnp.where(
            core == 0, jnp.concatenate([mine, other], axis=-1), jnp.concatenate([other, mine], axis=-1)
        )

    input_grad = whole(grad_own, grad_back).reshape(per_device, cell_count, channels)
    kernel_sum = own_part + last_swap.astype(jnp.float32) + mid_sum.astype(jnp.float32)
    kernel_mine = kernel_sum.astype(jnp.bfloat16)
    kernel_other = lax.ppermute(kernel_mine, "dp", SWAP)
    weight_grad = whole(kernel_mine, kernel_other).astype(jnp.float32) / per_device
    return (input_grad[None], weight_grad[None, None])


def solution(mesh):
    placed = (
        P("segment", ("expert", "dp"), None, None),
        P("segment", ("expert", "dp"), None, None),
        P("segment", ("expert", "dp"), None),
        P("segment", ("expert", "dp"), None),
        P("segment", "expert", None, None, None),
    )
    step = weights_travel if fits_line(mesh) else body
    return jax.shard_map(
        step,
        mesh=mesh,
        in_specs=placed,
        out_specs=(
            P("segment", ("expert", "dp"), None, None),
            P("segment", "expert", None, None, None),
        ),
        check_vma=False,
    )
```

```python
import jax
import jax.numpy as jnp
import numpy as np
from jax import lax
from jax.experimental import pallas as pl
from jax.experimental.pallas import tpu as pltpu
from jax.sharding import PartitionSpec as P

TH = 4
TW = 2


def shifted(array, axis, by):
    count = lax.axis_size(axis)
    return lax.ppermute(array, axis, [(i, (i + by) % count) for i in range(count)])


def offsets_table():
    cell_count = TH * TW
    table = np.zeros((cell_count, cell_count, 9), np.float32)
    for source_cell in range(cell_count):
        for target_cell in range(cell_count):
            row_step = target_cell // TW - source_cell // TW
            col_step = target_cell % TW - source_cell % TW
            if abs(row_step) <= 1 and abs(col_step) <= 1:
                table[source_cell, target_cell, (row_step + 1) * 3 + col_step + 1] = 1.0
    return table


def by_group(rows, group_width):
    tile_count = rows.shape[0]
    cell_count = rows.shape[1]
    group_count = rows.shape[2] // group_width
    split = rows.reshape(tile_count, cell_count, group_count, group_width).transpose(2, 0, 1, 3)
    return split.reshape(group_count, tile_count, cell_count * group_width)


def transpose_conv(scaled_grads, weight):
    tile_count = scaled_grads.shape[0]
    cell_count = scaled_grads.shape[1]
    group_width = weight.shape[1]
    channels = weight.shape[2]
    group_count = channels // group_width
    selector = jnp.asarray(offsets_table(), jnp.bfloat16)
    split_weight = weight.reshape(9, group_width, group_count, group_width)
    blocks = jnp.einsum(
        "pqt,tcgo->gpoqc", selector, split_weight, preferred_element_type=jnp.float32
    )
    blocks = blocks.astype(jnp.bfloat16).reshape(
        group_count, cell_count * group_width, cell_count * group_width
    )
    grouped = by_group(scaled_grads, group_width)
    result = jnp.einsum("gnk,gkm->gnm", grouped, blocks, preferred_element_type=jnp.float32)
    result = result.reshape(group_count, tile_count, cell_count, group_width).transpose(1, 2, 0, 3)
    return result.reshape(tile_count, cell_count, channels)


def weight_corr(inputs, scaled_grads, group_width):
    cell_count = inputs.shape[1]
    channels = inputs.shape[2]
    group_count = channels // group_width
    grouped_inputs = by_group(inputs, group_width)
    grouped_grads = by_group(scaled_grads, group_width)
    moments = jnp.einsum(
        "gnk,gnm->gkm", grouped_inputs, grouped_grads, preferred_element_type=jnp.float32
    )
    moments = moments.reshape(group_count, cell_count, group_width, cell_count, group_width)
    selector = jnp.asarray(offsets_table(), jnp.float32)
    taps = jnp.einsum("gpcqo,qpt->tcgo", moments, selector, precision=lax.Precision.HIGHEST)
    return taps.reshape(9, group_width, channels)


def body(activations, upstream, routes, gate_codes, weights):
    incoming = shifted(upstream, "segment", -1)[0]
    inputs = activations[0]
    route_ids = routes[0]
    code_values = gate_codes[0].astype(jnp.float32)
    kernel = weights[0, 0]
    group_width = kernel.shape[1]
    per_device = inputs.shape[0]
    cell_count = inputs.shape[1]
    channels = inputs.shape[2]
    experts = lax.axis_size("expert")
    capacity = max(2, 4 * per_device // experts)
    gate_share = code_values / jnp.sum(code_values, axis=1, keepdims=True)
    scaled_grads = (gate_share[:, :, None, None] * incoming[:, None].astype(jnp.float32)).astype(
        jnp.bfloat16
    )
    grad_rows = scaled_grads.reshape(2 * per_device, cell_count * channels)
    input_rows = jnp.repeat(inputs, 2, axis=0).reshape(2 * per_device, cell_count * channels)
    flat_expert = route_ids.reshape(-1)
    matches = (flat_expert[:, None] == jnp.arange(experts, dtype=jnp.int32)[None, :]).astype(
        jnp.int32
    )
    earlier = jnp.cumsum(matches, axis=0) - matches
    slot_rank = jnp.sum(earlier * matches, axis=1)
    slot_place = flat_expert * capacity + slot_rank
    chooser = (
        slot_place[None, :] == jnp.arange(experts * capacity, dtype=jnp.int32)[:, None]
    ).astype(jnp.bfloat16)

    def pack_slots(rows):
        packed = jnp.dot(chooser, rows, preferred_element_type=jnp.float32).astype(jnp.bfloat16)
        return packed.reshape(experts, capacity, cell_count, channels)

    inputs_recv, grads_recv = (
        lax.all_to_all(pack_slots(input_rows), "expert", split_axis=0, concat_axis=0, tiled=True),
        lax.all_to_all(pack_slots(grad_rows), "expert", split_axis=0, concat_axis=0, tiled=True),
    )
    flat_grads = grads_recv.reshape(experts * capacity, cell_count, channels)
    answers = transpose_conv(flat_grads, kernel).astype(jnp.bfloat16)
    returned = lax.all_to_all(
        answers.reshape(experts, capacity, cell_count, channels),
        "expert",
        split_axis=0,
        concat_axis=0,
        tiled=True,
    )
    flat_inputs = inputs_recv.reshape(experts * capacity, cell_count, channels)
    local_grad = weight_corr(flat_inputs, flat_grads, group_width)
    flat_answers = returned.reshape(experts * capacity, cell_count * channels)
    per_route = jnp.dot(chooser.T, flat_answers, preferred_element_type=jnp.float32).reshape(
        per_device, 2, cell_count, channels
    )
    input_grad = (incoming.astype(jnp.float32) + per_route[:, 0] + per_route[:, 1]).astype(
        jnp.bfloat16
    )
    total_grad = lax.psum(local_grad, "dp") / per_device
    return (input_grad[None], total_grad[None, None])


LINE = 4
CORES = 2
NEAR_PAIRS = [(0, 1), (1, 0), (2, 3), (3, 2)]
SWAP = [(0, 1), (1, 0)]
VMEM_LIMIT = 16 * 1024 * 1024


def inner_pairs():
    crossing = {1: 2, 2: 1}
    pairs = []
    for e in range(LINE):
        for d in range(CORES):
            target = (crossing[e], d) if e in crossing else (e, 1 - d)
            pairs.append((CORES * e + d, CORES * target[0] + target[1]))
    return pairs


def fits_line(mesh):
    return mesh.shape["expert"] == LINE and mesh.shape["dp"] == CORES


def cell_order():
    return [row * TW + col for col in range(TW) for row in range(TH)]


def own_gates(info, expert):
    codes = info[2:4].astype(jnp.float32)
    hits = jnp.where(info[0:2] == expert, codes, 0.0)
    return (hits[0:1] + hits[1:2]) / (codes[0:1] + codes[1:2])


def gate_columns(info_ref, experts):
    rows = [own_gates(info_ref[...], expert) for expert in experts]
    count = rows[0].shape[1]
    table = jnp.concatenate(rows + [jnp.zeros((8 - len(rows), count), jnp.float32)], axis=0)
    table = jnp.concatenate([table, jnp.zeros((8, 128 - count), jnp.float32)], axis=1)
    return table.T[:count]


def slot_experts():
    me = lax.axis_index("expert")
    outer = (me == 0) | (me == 3)
    mid = jnp.where(outer, 2, 3)
    far = 5 - mid
    return [me, me ^ 1, me ^ mid, me ^ far]


def prepare_kernel(grad_a, grad_b, act_a, act_b, info_a, info_b, scaled_ref, turned, far_ref, wide, cells):
    tiles = info_a.shape[1]
    block = 2 * tiles
    width = grad_a.shape[1]
    column = TH * block
    strips = width // 128
    for at, ref in enumerate((grad_a, grad_b, act_a, act_b)):
        for strip in range(strips):
            wide[at * strips + strip] = ref[:, pl.ds(strip * 128, 128)].astype(jnp.float32)

    def cell_rows(at, cell):
        pieces = [wide[at * strips + strip, pl.ds(cell, tiles, stride=TH * TW), :] for strip in range(strips)]
        return jnp.concatenate(pieces, axis=1)

    experts = slot_experts()
    gates_a = gate_columns(info_a, experts)
    gates_b = gate_columns(info_b, experts)
    for place, cell in enumerate(cell_order()):
        part_a = cell_rows(0, cell)
        part_b = cell_rows(1, cell)
        for slot in range(4):
            both = jnp.concatenate(
                [part_a * gates_a[:, slot : slot + 1], part_b * gates_b[:, slot : slot + 1]], axis=0
            )
            scaled_ref[slot, pl.ds(place * block, block), :] = both.astype(jnp.bfloat16)
        act_rows = jnp.concatenate([cell_rows(2, cell), cell_rows(3, cell)], axis=0)
        cells[pl.ds(place * block, block), :] = act_rows.astype(jnp.bfloat16)
    empty = jnp.zeros((block, width), jnp.bfloat16)
    for col in range(TW):
        rows = cells[pl.ds(col * column, column), :]
        turned[1, :, pl.ds(col * column, column)] = rows.T
        turned[2, :, pl.ds(col * column, column)] = jnp.concatenate([rows[block:], empty], axis=0).T
        turned[0, :, pl.ds(col * column, column)] = jnp.concatenate([empty, rows[:-block]], axis=0).T
    kernel_gradient(turned, scaled_ref, 3, far_ref)


def kernel_gradient(turned, scaled_ref, slot, ref):
    width, column = turned.shape[1], turned.shape[2] // TW
    low_half = lax.broadcasted_iota(jnp.int32, (64, 128), 1) < 64
    for row_off in (-1, 0, 1):
        for col_off in (-1, 0, 1):
            lhs = turned[row_off + 1]
            rhs = scaled_ref[slot]
            if col_off == 1:
                lhs, rhs = lhs[:, column:], rhs[:column]
            if col_off == -1:
                lhs, rhs = lhs[:, :column], rhs[column:]
            full = jnp.dot(lhs, rhs, preferred_element_type=jnp.float32)
            tap = (row_off + 1) * 3 + col_off + 1
            for pair in range(width // 128):
                base = pair * 128
                piece = jnp.where(
                    low_half,
                    full[base : base + 64, base : base + 128],
                    full[base + 64 : base + 128, base : base + 128],
                )
                ref[tap, :, pl.ds(base, 128)] = piece.astype(ref.dtype)


def partial_kernel(scaled_ref, turned, mid_ref, near_ref, own_ref):
    for slot, ref in ((2, mid_ref), (1, near_ref), (0, own_ref)):
        kernel_gradient(turned, scaled_ref, slot, ref)


def add_answers(scaled_ref, slots, kernels, total):
    width = total.shape[1]
    block = total.shape[0] // (TH * TW)
    lane_group = lax.broadcasted_iota(jnp.int32, (64, width), 1) // 64
    masks = [jnp.where(lane_group == g, 1.0, 0.0).astype(jnp.bfloat16) for g in range(width // 64)]
    for slot, ref in zip(slots, kernels):
        for row_off in (-1, 0, 1):
            for col_off in (-1, 0, 1):
                tap = (row_off + 1) * 3 + col_off + 1
                kernel = ref[tap]
                blocks = jnp.concatenate([kernel * mask for mask in masks], axis=0)
                first = max(0, -row_off)
                rows = (TH - abs(row_off)) * block
                for col in range(TW):
                    if not 0 <= col + col_off < TW:
                        continue
                    source = (col * TH + first) * block
                    target = ((col + col_off) * TH + first + row_off) * block
                    total[pl.ds(target, rows), :] += lax.dot_general(
                        scaled_ref[slot, pl.ds(source, rows), :],
                        blocks,
                        (((1,), (1,)), ((), ())),
                        preferred_element_type=jnp.float32,
                    )


def early_answer_kernel(scaled_ref, own_ref, near_ref, mid_ref, total):
    total[...] = jnp.zeros_like(total)
    add_answers(scaled_ref, (0, 1, 2), (own_ref, near_ref, mid_ref), total)


def late_answer_kernel(scaled_ref, far_ref, early, grad_a, grad_b, out_a, out_b, total, spread):
    tiles = grad_a.shape[0] // (TH * TW)
    block = 2 * tiles
    strips = grad_a.shape[1] // 128
    total[...] = early[...]
    add_answers(scaled_ref, (3,), (far_ref,), total)
    for at, (grad, out) in enumerate(((grad_a, out_a), (grad_b, out_b))):
        for strip in range(strips):
            lanes = pl.ds(strip * 128, 128)
            for place, cell in enumerate(cell_order()):
                spread[strip, pl.ds(cell, tiles, stride=TH * TW), :] = total[
                    pl.ds(place * block + at * tiles, tiles), lanes
                ]
            out[:, lanes] = (grad[:, lanes].astype(jnp.float32) + spread[strip]).astype(jnp.bfloat16)


def on_vmem(count):
    return [pl.BlockSpec(memory_space=pltpu.VMEM)] * count


def local_call(kernel, outs, scratch, flops, *operands):
    return pl.pallas_call(
        kernel,
        out_shape=tuple(outs),
        in_specs=on_vmem(len(operands)),
        out_specs=tuple(on_vmem(len(outs))),
        scratch_shapes=scratch,
        compiler_params=pltpu.CompilerParams(vmem_limit_bytes=VMEM_LIMIT),
        cost_estimate=pl.CostEstimate(flops=flops, bytes_accessed=2_000_000, transcendentals=0),
    )(*operands)


def weights_travel(activations, upstream, routes, gate_codes, weights):
    me = lax.axis_index("expert")
    core = lax.axis_index("dp")
    inner = (me == 1) | (me == 2)
    per_device, cell_count, channels = activations.shape[1:]
    rows = per_device * cell_count
    width = channels // 2
    kernel = weights[0, 0]
    taps, group_width = kernel.shape[0], kernel.shape[1]
    sections = lax.axis_size("segment")

    def half(array, which):
        return lax.dynamic_slice_in_dim(array, which * width, width, array.ndim - 1)

    def near(array):
        return lax.ppermute(array, "expert", NEAR_PAIRS)

    def across(array):
        return lax.ppermute(array, ("expert", "dp"), inner_pairs())

    def from_next(array, flip):
        pairs = []
        for s in range(sections):
            for d in range(2):
                pairs.append((2 * ((s + 1) % sections) + d, 2 * s + (1 - d if flip else d)))
        return lax.ppermute(array, ("segment", "dp"), pairs)

    info = jnp.concatenate([routes[0].T, gate_codes[0].T], axis=0)
    my_weights = half(kernel, core)
    my_weights, upstream = lax.optimization_barrier((my_weights, upstream))
    upstream_rows = upstream[0].reshape(rows, channels)
    act_rows = activations[0].reshape(rows, channels)
    inner_weights = across(my_weights)
    near_weights = near(my_weights)
    grad_a = from_next(half(upstream_rows, core), False)
    grad_b = from_next(half(upstream_rows, 1 - core), True)
    act_a = half(act_rows, core)
    act_b = lax.ppermute(half(act_rows, 1 - core), "dp", SWAP)
    info_b = lax.ppermute(info, "dp", SWAP)

    part = jax.ShapeDtypeStruct((taps, group_width, width), jnp.bfloat16)
    scaled, turned, far_part = local_call(
        prepare_kernel,
        (
            jax.ShapeDtypeStruct((4, 2 * rows, width), jnp.bfloat16),
            jax.ShapeDtypeStruct((3, width, 2 * rows), jnp.bfloat16),
            part,
        ),
        [
            pltpu.VMEM((4 * (width // 128), rows, 128), jnp.float32),
            pltpu.VMEM((2 * rows, width), jnp.bfloat16),
        ],
        800_000_000,
        grad_a, grad_b, act_a, act_b, info, info_b,
    )
    cross_weights = across(near_weights)
    first_swap = near(jnp.where(inner, inner_weights, far_part))
    mid_part, near_part, own_part = local_call(
        partial_kernel,
        (part, part, jax.ShapeDtypeStruct((taps, group_width, width), jnp.float32)),
        [],
        1_200_000_000,
        scaled, turned,
    )
    second_swap = near(jnp.where(inner, cross_weights, mid_part))
    far_sum = across(far_part + first_swap)
    mid_sum = across(mid_part + second_swap)
    last_swap = near(jnp.where(inner, near_part + far_sum, near_part))

    mid_weights = jnp.where(inner, inner_weights, first_swap)
    far_weights = jnp.where(inner, cross_weights, second_swap)
    (early,) = local_call(
        early_answer_kernel,
        (jax.ShapeDtypeStruct((2 * rows, width), jnp.float32),),
        [],
        1_200_000_000,
        scaled, my_weights, near_weights, mid_weights,
    )
    answer = jax.ShapeDtypeStruct((rows, width), jnp.bfloat16)
    grad_own, grad_other = local_call(
        late_answer_kernel,
        (answer, answer),
        [
            pltpu.VMEM((2 * rows, width), jnp.float32),
            pltpu.VMEM((width // 128, rows, 128), jnp.float32),
        ],
        500_000_000,
        scaled, far_weights, early, grad_a, grad_b,
    )
    grad_back = lax.ppermute(grad_other, "dp", SWAP)

    def whole(mine, other):
        return jnp.where(
            core == 0, jnp.concatenate([mine, other], axis=-1), jnp.concatenate([other, mine], axis=-1)
        )

    input_grad = whole(grad_own, grad_back).reshape(per_device, cell_count, channels)
    last_swap, input_grad = lax.optimization_barrier((last_swap, input_grad))
    kernel_sum = own_part + last_swap.astype(jnp.float32) + jnp.where(inner, mid_sum, 0).astype(jnp.float32)
    kernel_mine = kernel_sum.astype(jnp.bfloat16)
    kernel_other = lax.ppermute(kernel_mine, "dp", SWAP)
    weight_grad = whole(kernel_mine, kernel_other).astype(jnp.float32) / per_device
    return (input_grad[None], weight_grad[None, None])


def solution(mesh):
    placed = (
        P("segment", ("expert", "dp"), None, None),
        P("segment", ("expert", "dp"), None, None),
        P("segment", ("expert", "dp"), None),
        P("segment", ("expert", "dp"), None),
        P("segment", "expert", None, None, None),
    )
    step = weights_travel if fits_line(mesh) else body
    return jax.shard_map(
        step,
        mesh=mesh,
        in_specs=placed,
        out_specs=(
            P("segment", ("expert", "dp"), None, None),
            P("segment", "expert", None, None, None),
        ),
        check_vma=False,
    )
```

```python
import functools

import jax
import jax.numpy as jnp
import numpy as np
from jax import lax
from jax.experimental import pallas as pl
from jax.experimental.pallas import tpu as pltpu
from jax.sharding import PartitionSpec as P

TH = 4
TW = 2


def shifted(array, axis, by):
    count = lax.axis_size(axis)
    return lax.ppermute(array, axis, [(i, (i + by) % count) for i in range(count)])


def offsets_table():
    cell_count = TH * TW
    table = np.zeros((cell_count, cell_count, 9), np.float32)
    for source_cell in range(cell_count):
        for target_cell in range(cell_count):
            row_step = target_cell // TW - source_cell // TW
            col_step = target_cell % TW - source_cell % TW
            if abs(row_step) <= 1 and abs(col_step) <= 1:
                table[source_cell, target_cell, (row_step + 1) * 3 + col_step + 1] = 1.0
    return table


def by_group(rows, group_width):
    tile_count = rows.shape[0]
    cell_count = rows.shape[1]
    group_count = rows.shape[2] // group_width
    split = rows.reshape(tile_count, cell_count, group_count, group_width).transpose(2, 0, 1, 3)
    return split.reshape(group_count, tile_count, cell_count * group_width)


def transpose_conv(scaled_grads, weight):
    tile_count = scaled_grads.shape[0]
    cell_count = scaled_grads.shape[1]
    group_width = weight.shape[1]
    channels = weight.shape[2]
    group_count = channels // group_width
    selector = jnp.asarray(offsets_table(), jnp.bfloat16)
    split_weight = weight.reshape(9, group_width, group_count, group_width)
    blocks = jnp.einsum(
        "pqt,tcgo->gpoqc", selector, split_weight, preferred_element_type=jnp.float32
    )
    blocks = blocks.astype(jnp.bfloat16).reshape(
        group_count, cell_count * group_width, cell_count * group_width
    )
    grouped = by_group(scaled_grads, group_width)
    result = jnp.einsum("gnk,gkm->gnm", grouped, blocks, preferred_element_type=jnp.float32)
    result = result.reshape(group_count, tile_count, cell_count, group_width).transpose(1, 2, 0, 3)
    return result.reshape(tile_count, cell_count, channels)


def weight_corr(inputs, scaled_grads, group_width):
    cell_count = inputs.shape[1]
    channels = inputs.shape[2]
    group_count = channels // group_width
    grouped_inputs = by_group(inputs, group_width)
    grouped_grads = by_group(scaled_grads, group_width)
    moments = jnp.einsum(
        "gnk,gnm->gkm", grouped_inputs, grouped_grads, preferred_element_type=jnp.float32
    )
    moments = moments.reshape(group_count, cell_count, group_width, cell_count, group_width)
    selector = jnp.asarray(offsets_table(), jnp.float32)
    taps = jnp.einsum("gpcqo,qpt->tcgo", moments, selector, precision=lax.Precision.HIGHEST)
    return taps.reshape(9, group_width, channels)


def body(activations, upstream, routes, gate_codes, weights):
    incoming = shifted(upstream, "segment", -1)[0]
    inputs = activations[0]
    route_ids = routes[0]
    code_values = gate_codes[0].astype(jnp.float32)
    kernel = weights[0, 0]
    group_width = kernel.shape[1]
    per_device = inputs.shape[0]
    cell_count = inputs.shape[1]
    channels = inputs.shape[2]
    experts = lax.axis_size("expert")
    capacity = max(2, 4 * per_device // experts)
    gate_share = code_values / jnp.sum(code_values, axis=1, keepdims=True)
    scaled_grads = (gate_share[:, :, None, None] * incoming[:, None].astype(jnp.float32)).astype(
        jnp.bfloat16
    )
    grad_rows = scaled_grads.reshape(2 * per_device, cell_count * channels)
    input_rows = jnp.repeat(inputs, 2, axis=0).reshape(2 * per_device, cell_count * channels)
    flat_expert = route_ids.reshape(-1)
    matches = (flat_expert[:, None] == jnp.arange(experts, dtype=jnp.int32)[None, :]).astype(
        jnp.int32
    )
    earlier = jnp.cumsum(matches, axis=0) - matches
    slot_rank = jnp.sum(earlier * matches, axis=1)
    slot_place = flat_expert * capacity + slot_rank
    chooser = (
        slot_place[None, :] == jnp.arange(experts * capacity, dtype=jnp.int32)[:, None]
    ).astype(jnp.bfloat16)

    def pack_slots(rows):
        packed = jnp.dot(chooser, rows, preferred_element_type=jnp.float32).astype(jnp.bfloat16)
        return packed.reshape(experts, capacity, cell_count, channels)

    inputs_recv, grads_recv = (
        lax.all_to_all(pack_slots(input_rows), "expert", split_axis=0, concat_axis=0, tiled=True),
        lax.all_to_all(pack_slots(grad_rows), "expert", split_axis=0, concat_axis=0, tiled=True),
    )
    flat_grads = grads_recv.reshape(experts * capacity, cell_count, channels)
    answers = transpose_conv(flat_grads, kernel).astype(jnp.bfloat16)
    returned = lax.all_to_all(
        answers.reshape(experts, capacity, cell_count, channels),
        "expert",
        split_axis=0,
        concat_axis=0,
        tiled=True,
    )
    flat_inputs = inputs_recv.reshape(experts * capacity, cell_count, channels)
    local_grad = weight_corr(flat_inputs, flat_grads, group_width)
    flat_answers = returned.reshape(experts * capacity, cell_count * channels)
    per_route = jnp.dot(chooser.T, flat_answers, preferred_element_type=jnp.float32).reshape(
        per_device, 2, cell_count, channels
    )
    input_grad = (incoming.astype(jnp.float32) + per_route[:, 0] + per_route[:, 1]).astype(
        jnp.bfloat16
    )
    total_grad = lax.psum(local_grad, "dp") / per_device
    return (input_grad[None], total_grad[None, None])


LINE = 4
CORES = 2
NEAR_PAIRS = [(0, 1), (1, 0), (2, 3), (3, 2)]
SWAP = [(0, 1), (1, 0)]
VMEM_LIMIT = 16 * 1024 * 1024


def inner_pairs():
    crossing = {1: 2, 2: 1}
    pairs = []
    for e in range(LINE):
        for d in range(CORES):
            target = (crossing[e], d) if e in crossing else (e, 1 - d)
            pairs.append((CORES * e + d, CORES * target[0] + target[1]))
    return pairs


def fits_line(mesh):
    return mesh.shape["expert"] == LINE and mesh.shape["dp"] == CORES


def cell_order():
    return [row * TW + col for col in range(TW) for row in range(TH)]


def own_gates(info, expert):
    codes = info[2:4].astype(jnp.float32)
    hits = jnp.where(info[0:2] == expert, codes, 0.0)
    return (hits[0:1] + hits[1:2]) / (codes[0:1] + codes[1:2])


def gate_columns(info_ref, experts):
    rows = [own_gates(info_ref[...], expert) for expert in experts]
    count = rows[0].shape[1]
    table = jnp.concatenate(rows + [jnp.zeros((8 - len(rows), count), jnp.float32)], axis=0)
    table = jnp.concatenate([table, jnp.zeros((8, 128 - count), jnp.float32)], axis=1)
    return table.T[:count]


def slot_experts():
    me = lax.axis_index("expert")
    outer = (me == 0) | (me == 3)
    mid = jnp.where(outer, 2, 3)
    far = 5 - mid
    return [me, me ^ 1, me ^ mid, me ^ far]


def prepare_kernel(grad_a, grad_b, act_a, act_b, info_a, info_b, scaled_ref, turned, far_ref, wide, cells):
    tiles = info_a.shape[1]
    block = 2 * tiles
    width = grad_a.shape[1]
    column = TH * block
    strips = width // 128
    for at, ref in enumerate((grad_a, grad_b, act_a, act_b)):
        for strip in range(strips):
            wide[at * strips + strip] = ref[:, pl.ds(strip * 128, 128)].astype(jnp.float32)

    def cell_rows(at, cell):
        pieces = [wide[at * strips + strip, pl.ds(cell, tiles, stride=TH * TW), :] for strip in range(strips)]
        return jnp.concatenate(pieces, axis=1)

    experts = slot_experts()
    gates_a = gate_columns(info_a, experts)
    gates_b = gate_columns(info_b, experts)
    for place, cell in enumerate(cell_order()):
        part_a = cell_rows(0, cell)
        part_b = cell_rows(1, cell)
        for slot in range(4):
            both = jnp.concatenate(
                [part_a * gates_a[:, slot : slot + 1], part_b * gates_b[:, slot : slot + 1]], axis=0
            )
            scaled_ref[slot, pl.ds(place * block, block), :] = both.astype(jnp.bfloat16)
        act_rows = jnp.concatenate([cell_rows(2, cell), cell_rows(3, cell)], axis=0)
        cells[pl.ds(place * block, block), :] = act_rows.astype(jnp.bfloat16)
    empty = jnp.zeros((block, width), jnp.bfloat16)
    for col in range(TW):
        rows = cells[pl.ds(col * column, column), :]
        turned[1, :, pl.ds(col * column, column)] = rows.T
        turned[2, :, pl.ds(col * column, column)] = jnp.concatenate([rows[block:], empty], axis=0).T
        turned[0, :, pl.ds(col * column, column)] = jnp.concatenate([empty, rows[:-block]], axis=0).T
    kernel_gradient(turned, scaled_ref, 3, far_ref)


def kernel_gradient(turned, scaled_ref, slot, ref):
    width, column = turned.shape[1], turned.shape[2] // TW
    low_half = lax.broadcasted_iota(jnp.int32, (64, 128), 1) < 64
    for row_off in (-1, 0, 1):
        for col_off in (-1, 0, 1):
            lhs = turned[row_off + 1]
            rhs = scaled_ref[slot]
            if col_off == 1:
                lhs, rhs = lhs[:, column:], rhs[:column]
            if col_off == -1:
                lhs, rhs = lhs[:, :column], rhs[column:]
            full = jnp.dot(lhs, rhs, preferred_element_type=jnp.float32)
            tap = (row_off + 1) * 3 + col_off + 1
            for pair in range(width // 128):
                base = pair * 128
                piece = jnp.where(
                    low_half,
                    full[base : base + 64, base : base + 128],
                    full[base + 64 : base + 128, base : base + 128],
                )
                ref[tap, :, pl.ds(base, 128)] = piece.astype(ref.dtype)


def partial_kernel(scaled_ref, turned, mid_ref, near_ref, own_ref):
    for slot, ref in ((2, mid_ref), (1, near_ref), (0, own_ref)):
        kernel_gradient(turned, scaled_ref, slot, ref)


def add_answers(scaled_ref, slots, kernels, total):
    width = total.shape[1]
    block = total.shape[0] // (TH * TW)
    lane_group = lax.broadcasted_iota(jnp.int32, (64, width), 1) // 64
    masks = [jnp.where(lane_group == g, 1.0, 0.0).astype(jnp.bfloat16) for g in range(width // 64)]
    for slot, ref in zip(slots, kernels):
        for row_off in (-1, 0, 1):
            for col_off in (-1, 0, 1):
                tap = (row_off + 1) * 3 + col_off + 1
                kernel = ref[tap]
                blocks = jnp.concatenate([kernel * mask for mask in masks], axis=0)
                first = max(0, -row_off)
                rows = (TH - abs(row_off)) * block
                for col in range(TW):
                    if not 0 <= col + col_off < TW:
                        continue
                    source = (col * TH + first) * block
                    target = ((col + col_off) * TH + first + row_off) * block
                    total[pl.ds(target, rows), :] += lax.dot_general(
                        scaled_ref[slot, pl.ds(source, rows), :],
                        blocks,
                        (((1,), (1,)), ((), ())),
                        preferred_element_type=jnp.float32,
                    )


def early_answer_kernel(scaled_ref, own_ref, near_ref, mid_ref, total):
    total[...] = jnp.zeros_like(total)
    add_answers(scaled_ref, (0, 1, 2), (own_ref, near_ref, mid_ref), total)


def late_answer_kernel(scaled_ref, far_ref, early, grad_a, grad_b, out_a, out_b, total, spread):
    tiles = grad_a.shape[0] // (TH * TW)
    block = 2 * tiles
    strips = grad_a.shape[1] // 128
    total[...] = early[...]
    add_answers(scaled_ref, (3,), (far_ref,), total)
    for at, (grad, out) in enumerate(((grad_a, out_a), (grad_b, out_b))):
        for strip in range(strips):
            lanes = pl.ds(strip * 128, 128)
            for place, cell in enumerate(cell_order()):
                spread[strip, pl.ds(cell, tiles, stride=TH * TW), :] = total[
                    pl.ds(place * block + at * tiles, tiles), lanes
                ]
            out[:, lanes] = (grad[:, lanes].astype(jnp.float32) + spread[strip]).astype(jnp.bfloat16)


def place_half_kernel(scale, side, core_ref, half_ref, *refs):
    out, staged, done = refs[-3:]
    taps, _, width = half_ref.shape
    at = core_ref[0] if side == 0 else 1 - core_ref[0]
    lanes = pl.ds(pl.multiple_of(at * width, width), width)
    copies = []
    for tap in range(taps):
        staged[tap] = half_ref[tap].astype(jnp.float32) * scale
        copies.append(pltpu.make_async_copy(staged.at[tap], out.at[tap, :, lanes], done.at[tap]))
        copies[-1].start()
    for copy in copies:
        copy.wait()


def place_half(scale, side, core_at, half, begun=None):
    taps, group_width, width = half.shape
    specs = [pl.BlockSpec(memory_space=pltpu.SMEM)] + on_vmem(1)
    operands = [core_at, half]
    if begun is not None:
        specs.append(pl.BlockSpec(memory_space=pl.ANY))
        operands.append(begun)
    return pl.pallas_call(
        functools.partial(place_half_kernel, scale, side),
        out_shape=jax.ShapeDtypeStruct((taps, group_width, 2 * width), jnp.float32),
        in_specs=specs,
        out_specs=pl.BlockSpec(memory_space=pl.ANY),
        scratch_shapes=[
            pltpu.VMEM((taps, group_width, width), jnp.float32),
            pltpu.SemaphoreType.DMA((taps,)),
        ],
        input_output_aliases={} if begun is None else {2: 0},
        compiler_params=pltpu.CompilerParams(vmem_limit_bytes=VMEM_LIMIT),
        cost_estimate=pl.CostEstimate(flops=1000, bytes_accessed=1000, transcendentals=0),
    )(*operands)


def on_vmem(count):
    return [pl.BlockSpec(memory_space=pltpu.VMEM)] * count


def local_call(kernel, outs, scratch, flops, *operands):
    return pl.pallas_call(
        kernel,
        out_shape=tuple(outs),
        in_specs=on_vmem(len(operands)),
        out_specs=tuple(on_vmem(len(outs))),
        scratch_shapes=scratch,
        compiler_params=pltpu.CompilerParams(vmem_limit_bytes=VMEM_LIMIT),
        cost_estimate=pl.CostEstimate(flops=1000, bytes_accessed=1000, transcendentals=0),
    )(*operands)


def weights_travel(activations, upstream, routes, gate_codes, weights):
    me = lax.axis_index("expert")
    core = lax.axis_index("dp")
    inner = (me == 1) | (me == 2)
    per_device, cell_count, channels = activations.shape[1:]
    rows = per_device * cell_count
    width = channels // 2
    taps, group_width = weights.shape[2:4]
    sections = lax.axis_size("segment")

    def half(array, which):
        return lax.dynamic_slice_in_dim(array, which * width, width, array.ndim - 1)

    def near(array):
        return lax.ppermute(array, "expert", NEAR_PAIRS)

    def across(array):
        return lax.ppermute(array, ("expert", "dp"), inner_pairs())

    def from_next(array):
        return lax.ppermute(array, "segment", [((s + 1) % sections, s) for s in range(sections)])

    info = jnp.concatenate([routes[0].T, gate_codes[0].T], axis=0)
    info_b = lax.ppermute(info, "dp", SWAP)
    grad_rows = from_next(upstream[0].reshape(rows, channels))
    my_weights = half(weights[0, 0], core)
    inner_weights = across(my_weights)
    act_rows = activations[0].reshape(rows, channels)
    act_a = half(act_rows, core)
    act_b = lax.ppermute(half(act_rows, 1 - core), "dp", SWAP)
    near_weights = near(my_weights)
    grad_a = half(grad_rows, core)
    grad_b = lax.ppermute(half(grad_rows, 1 - core), "dp", SWAP)

    part = jax.ShapeDtypeStruct((taps, group_width, width), jnp.bfloat16)
    scaled, turned, far_part = local_call(
        prepare_kernel,
        (
            jax.ShapeDtypeStruct((4, 2 * rows, width), jnp.bfloat16),
            jax.ShapeDtypeStruct((3, width, 2 * rows), jnp.bfloat16),
            part,
        ),
        [
            pltpu.VMEM((4 * (width // 128), rows, 128), jnp.float32),
            pltpu.VMEM((2 * rows, width), jnp.bfloat16),
        ],
        800_000_000,
        grad_a, grad_b, act_a, act_b, info, info_b,
    )
    near_weights, far_part = lax.optimization_barrier((near_weights, far_part))
    cross_weights = across(near_weights)
    first_swap = near(jnp.where(inner, inner_weights, far_part))
    mid_part, near_part, own_part = local_call(
        partial_kernel,
        (part, part, jax.ShapeDtypeStruct((taps, group_width, width), jnp.float32)),
        [],
        1_200_000_000,
        scaled, turned,
    )
    first_swap, mid_part = lax.optimization_barrier((first_swap, mid_part))
    second_swap = near(jnp.where(inner, cross_weights, mid_part))
    far_sum = across(far_part + first_swap)
    mid_sum = across(mid_part + second_swap)
    last_swap = near(jnp.where(inner, near_part + far_sum, near_part))

    mid_weights = jnp.where(inner, inner_weights, first_swap)
    far_weights = jnp.where(inner, cross_weights, second_swap)
    (early,) = local_call(
        early_answer_kernel,
        (jax.ShapeDtypeStruct((2 * rows, width), jnp.float32),),
        [],
        1_200_000_000,
        scaled, my_weights, near_weights, mid_weights,
    )
    answer = jax.ShapeDtypeStruct((rows, width), jnp.bfloat16)
    grad_own, grad_other = local_call(
        late_answer_kernel,
        (answer, answer),
        [
            pltpu.VMEM((2 * rows, width), jnp.float32),
            pltpu.VMEM((width // 128, rows, 128), jnp.float32),
        ],
        500_000_000,
        scaled, far_weights, early, grad_a, grad_b,
    )
    grad_back = lax.ppermute(grad_other, "dp", SWAP)

    def whole(mine, other):
        return jnp.where(
            core == 0, jnp.concatenate([mine, other], axis=-1), jnp.concatenate([other, mine], axis=-1)
        )

    input_grad = whole(grad_own, grad_back).reshape(per_device, cell_count, channels)
    last_swap, input_grad = lax.optimization_barrier((last_swap, input_grad))
    kernel_sum = own_part + last_swap.astype(jnp.float32) + jnp.where(inner, mid_sum, 0).astype(jnp.float32)
    kernel_mine = kernel_sum.astype(jnp.bfloat16)
    kernel_other = lax.ppermute(kernel_mine, "dp", SWAP)
    core_at = jnp.reshape(core, (1,)).astype(jnp.int32)
    begun = place_half(1.0 / per_device, 0, core_at, kernel_mine)
    weight_grad = place_half(1.0 / per_device, 1, core_at, kernel_other, begun)
    return (input_grad[None], weight_grad[None, None])


def solution(mesh):
    placed = (
        P("segment", ("expert", "dp"), None, None),
        P("segment", ("expert", "dp"), None, None),
        P("segment", ("expert", "dp"), None),
        P("segment", ("expert", "dp"), None),
        P("segment", "expert", None, None, None),
    )
    step = weights_travel if fits_line(mesh) else body
    return jax.shard_map(
        step,
        mesh=mesh,
        in_specs=placed,
        out_specs=(
            P("segment", ("expert", "dp"), None, None),
            P("segment", "expert", None, None, None),
        ),
        check_vma=False,
    )
```

```python
import functools

import jax
import jax.numpy as jnp
import numpy as np
from jax import lax
from jax.experimental import pallas as pl
from jax.experimental.pallas import tpu as pltpu
from jax.sharding import PartitionSpec as P

TH = 4
TW = 2


def shifted(array, axis, by):
    count = lax.axis_size(axis)
    return lax.ppermute(array, axis, [(i, (i + by) % count) for i in range(count)])


def offsets_table():
    cell_count = TH * TW
    table = np.zeros((cell_count, cell_count, 9), np.float32)
    for source_cell in range(cell_count):
        for target_cell in range(cell_count):
            row_step = target_cell // TW - source_cell // TW
            col_step = target_cell % TW - source_cell % TW
            if abs(row_step) <= 1 and abs(col_step) <= 1:
                table[source_cell, target_cell, (row_step + 1) * 3 + col_step + 1] = 1.0
    return table


def by_group(rows, group_width):
    tile_count = rows.shape[0]
    cell_count = rows.shape[1]
    group_count = rows.shape[2] // group_width
    split = rows.reshape(tile_count, cell_count, group_count, group_width).transpose(2, 0, 1, 3)
    return split.reshape(group_count, tile_count, cell_count * group_width)


def transpose_conv(scaled_grads, weight):
    tile_count = scaled_grads.shape[0]
    cell_count = scaled_grads.shape[1]
    group_width = weight.shape[1]
    channels = weight.shape[2]
    group_count = channels // group_width
    selector = jnp.asarray(offsets_table(), jnp.bfloat16)
    split_weight = weight.reshape(9, group_width, group_count, group_width)
    blocks = jnp.einsum(
        "pqt,tcgo->gpoqc", selector, split_weight, preferred_element_type=jnp.float32
    )
    blocks = blocks.astype(jnp.bfloat16).reshape(
        group_count, cell_count * group_width, cell_count * group_width
    )
    grouped = by_group(scaled_grads, group_width)
    result = jnp.einsum("gnk,gkm->gnm", grouped, blocks, preferred_element_type=jnp.float32)
    result = result.reshape(group_count, tile_count, cell_count, group_width).transpose(1, 2, 0, 3)
    return result.reshape(tile_count, cell_count, channels)


def weight_corr(inputs, scaled_grads, group_width):
    cell_count = inputs.shape[1]
    channels = inputs.shape[2]
    group_count = channels // group_width
    grouped_inputs = by_group(inputs, group_width)
    grouped_grads = by_group(scaled_grads, group_width)
    moments = jnp.einsum(
        "gnk,gnm->gkm", grouped_inputs, grouped_grads, preferred_element_type=jnp.float32
    )
    moments = moments.reshape(group_count, cell_count, group_width, cell_count, group_width)
    selector = jnp.asarray(offsets_table(), jnp.float32)
    taps = jnp.einsum("gpcqo,qpt->tcgo", moments, selector, precision=lax.Precision.HIGHEST)
    return taps.reshape(9, group_width, channels)


def body(activations, upstream, routes, gate_codes, weights):
    incoming = shifted(upstream, "segment", -1)[0]
    inputs = activations[0]
    route_ids = routes[0]
    code_values = gate_codes[0].astype(jnp.float32)
    kernel = weights[0, 0]
    group_width = kernel.shape[1]
    per_device = inputs.shape[0]
    cell_count = inputs.shape[1]
    channels = inputs.shape[2]
    experts = lax.axis_size("expert")
    capacity = max(2, 4 * per_device // experts)
    gate_share = code_values / jnp.sum(code_values, axis=1, keepdims=True)
    scaled_grads = (gate_share[:, :, None, None] * incoming[:, None].astype(jnp.float32)).astype(
        jnp.bfloat16
    )
    grad_rows = scaled_grads.reshape(2 * per_device, cell_count * channels)
    input_rows = jnp.repeat(inputs, 2, axis=0).reshape(2 * per_device, cell_count * channels)
    flat_expert = route_ids.reshape(-1)
    matches = (flat_expert[:, None] == jnp.arange(experts, dtype=jnp.int32)[None, :]).astype(
        jnp.int32
    )
    earlier = jnp.cumsum(matches, axis=0) - matches
    slot_rank = jnp.sum(earlier * matches, axis=1)
    slot_place = flat_expert * capacity + slot_rank
    chooser = (
        slot_place[None, :] == jnp.arange(experts * capacity, dtype=jnp.int32)[:, None]
    ).astype(jnp.bfloat16)

    def pack_slots(rows):
        packed = jnp.dot(chooser, rows, preferred_element_type=jnp.float32).astype(jnp.bfloat16)
        return packed.reshape(experts, capacity, cell_count, channels)

    inputs_recv, grads_recv = (
        lax.all_to_all(pack_slots(input_rows), "expert", split_axis=0, concat_axis=0, tiled=True),
        lax.all_to_all(pack_slots(grad_rows), "expert", split_axis=0, concat_axis=0, tiled=True),
    )
    flat_grads = grads_recv.reshape(experts * capacity, cell_count, channels)
    answers = transpose_conv(flat_grads, kernel).astype(jnp.bfloat16)
    returned = lax.all_to_all(
        answers.reshape(experts, capacity, cell_count, channels),
        "expert",
        split_axis=0,
        concat_axis=0,
        tiled=True,
    )
    flat_inputs = inputs_recv.reshape(experts * capacity, cell_count, channels)
    local_grad = weight_corr(flat_inputs, flat_grads, group_width)
    flat_answers = returned.reshape(experts * capacity, cell_count * channels)
    per_route = jnp.dot(chooser.T, flat_answers, preferred_element_type=jnp.float32).reshape(
        per_device, 2, cell_count, channels
    )
    input_grad = (incoming.astype(jnp.float32) + per_route[:, 0] + per_route[:, 1]).astype(
        jnp.bfloat16
    )
    total_grad = lax.psum(local_grad, "dp") / per_device
    return (input_grad[None], total_grad[None, None])


LINE = 4
CORES = 2
NEAR_PAIRS = [(0, 1), (1, 0), (2, 3), (3, 2)]
SWAP = [(0, 1), (1, 0)]
VMEM_LIMIT = 16 * 1024 * 1024


def inner_pairs():
    crossing = {1: 2, 2: 1}
    pairs = []
    for e in range(LINE):
        for d in range(CORES):
            target = (crossing[e], d) if e in crossing else (e, 1 - d)
            pairs.append((CORES * e + d, CORES * target[0] + target[1]))
    return pairs


def fits_line(mesh):
    return mesh.shape["expert"] == LINE and mesh.shape["dp"] == CORES


def cell_order():
    return [row * TW + col for col in range(TW) for row in range(TH)]


def own_gates(info, expert):
    codes = info[2:4].astype(jnp.float32)
    hits = jnp.where(info[0:2] == expert, codes, 0.0)
    return (hits[0:1] + hits[1:2]) / (codes[0:1] + codes[1:2])


def gate_columns(info_ref, experts):
    rows = [own_gates(info_ref[...], expert) for expert in experts]
    count = rows[0].shape[1]
    table = jnp.concatenate(rows + [jnp.zeros((128 - len(rows), count), jnp.float32)], axis=0)
    table = jnp.concatenate([table, jnp.zeros((128, 128 - count), jnp.float32)], axis=1)
    return table.T[:count]


def slot_experts():
    me = lax.axis_index("expert")
    outer = (me == 0) | (me == 3)
    mid = jnp.where(outer, 2, 3)
    far = 5 - mid
    return [me, me ^ 1, me ^ mid, me ^ far]


def rows_by_cell(refs, wide):
    strips = refs[0].shape[1] // 128
    tiles = refs[0].shape[0] // (TH * TW)
    for at, ref in enumerate(refs):
        for strip in range(strips):
            wide[at * strips + strip] = ref[:, pl.ds(strip * 128, 128)].astype(jnp.float32)

    def cell_rows(at, cell):
        pieces = [wide[at * strips + strip, pl.ds(cell, tiles, stride=TH * TW), :] for strip in range(strips)]
        return jnp.concatenate(pieces, axis=1)

    return cell_rows


def turn_kernel(act_a, act_b, turned, wide, cells):
    width = act_a.shape[1]
    block = 2 * act_a.shape[0] // (TH * TW)
    column = TH * block
    cell_rows = rows_by_cell((act_a, act_b), wide)
    for place, cell in enumerate(cell_order()):
        act_rows = jnp.concatenate([cell_rows(0, cell), cell_rows(1, cell)], axis=0)
        cells[pl.ds(place * block, block), :] = act_rows.astype(jnp.bfloat16)
    empty = jnp.zeros((block, width), jnp.bfloat16)
    for col in range(TW):
        rows = cells[pl.ds(col * column, column), :]
        turned[1, :, pl.ds(col * column, column)] = rows.T
        turned[2, :, pl.ds(col * column, column)] = jnp.concatenate([rows[block:], empty], axis=0).T
        turned[0, :, pl.ds(col * column, column)] = jnp.concatenate([empty, rows[:-block]], axis=0).T


def prepare_kernel(grad_a, grad_b, turned, info_a, info_b, cells, gates, far_ref, wide, scaled):
    tiles = info_a.shape[1]
    block = 2 * tiles
    cell_rows = rows_by_cell((grad_a, grad_b), wide)
    experts = slot_experts()
    gates[pl.ds(0, tiles), :] = gate_columns(info_a, experts)
    gates[pl.ds(tiles, tiles), :] = gate_columns(info_b, experts)
    far_gate = gates[:, 3:4]
    for place, cell in enumerate(cell_order()):
        both = jnp.concatenate([cell_rows(0, cell), cell_rows(1, cell)], axis=0)
        cells[pl.ds(place * block, block), :] = both.astype(jnp.bfloat16)
        scaled[0, pl.ds(place * block, block), :] = (both * far_gate).astype(jnp.bfloat16)
    kernel_gradient(turned, scaled, 0, far_ref)


def kernel_gradient(turned, scaled_ref, slot, ref):
    width, column = turned.shape[1], turned.shape[2] // TW
    low_half = lax.broadcasted_iota(jnp.int32, (64, 128), 1) < 64
    for row_off in (-1, 0, 1):
        for col_off in (-1, 0, 1):
            lhs = turned[row_off + 1]
            rhs = scaled_ref[slot]
            if col_off == 1:
                lhs, rhs = lhs[:, column:], rhs[:column]
            if col_off == -1:
                lhs, rhs = lhs[:, :column], rhs[column:]
            full = jnp.dot(lhs, rhs, preferred_element_type=jnp.float32)
            tap = (row_off + 1) * 3 + col_off + 1
            for pair in range(width // 128):
                base = pair * 128
                piece = jnp.where(
                    low_half,
                    full[base : base + 64, base : base + 128],
                    full[base + 64 : base + 128, base : base + 128],
                )
                ref[tap, :, pl.ds(base, 128)] = piece.astype(ref.dtype)


def partial_kernel(cells, gates, turned, scaled_ref, mid_ref, near_ref, own_ref):
    block = gates.shape[0]
    for place in range(TH * TW):
        rows = cells[pl.ds(place * block, block), :].astype(jnp.float32)
        for slot in range(4):
            scaled_ref[slot, pl.ds(place * block, block), :] = (rows * gates[:, slot : slot + 1]).astype(jnp.bfloat16)
    for slot, ref in ((2, mid_ref), (1, near_ref), (0, own_ref)):
        kernel_gradient(turned, scaled_ref, slot, ref)


def add_answers(scaled_ref, slots, kernels, total):
    width = total.shape[1]
    block = total.shape[0] // (TH * TW)
    lane_group = lax.broadcasted_iota(jnp.int32, (64, width), 1) // 64
    masks = [jnp.where(lane_group == g, 1.0, 0.0).astype(jnp.bfloat16) for g in range(width // 64)]
    for slot, ref in zip(slots, kernels):
        for row_off in (-1, 0, 1):
            for col_off in (-1, 0, 1):
                tap = (row_off + 1) * 3 + col_off + 1
                kernel = ref[tap]
                blocks = jnp.concatenate([kernel * mask for mask in masks], axis=0)
                first = max(0, -row_off)
                rows = (TH - abs(row_off)) * block
                for col in range(TW):
                    if not 0 <= col + col_off < TW:
                        continue
                    source = (col * TH + first) * block
                    target = ((col + col_off) * TH + first + row_off) * block
                    total[pl.ds(target, rows), :] += lax.dot_general(
                        scaled_ref[slot, pl.ds(source, rows), :],
                        blocks,
                        (((1,), (1,)), ((), ())),
                        preferred_element_type=jnp.float32,
                    )


def early_answer_kernel(scaled_ref, own_ref, near_ref, mid_ref, total):
    total[...] = jnp.zeros_like(total)
    add_answers(scaled_ref, (0, 1, 2), (own_ref, near_ref, mid_ref), total)


def late_answer_kernel(scaled_ref, far_ref, early, grad_a, grad_b, out_a, out_b, total, spread):
    tiles = grad_a.shape[0] // (TH * TW)
    block = 2 * tiles
    strips = grad_a.shape[1] // 128
    total[...] = early[...]
    add_answers(scaled_ref, (3,), (far_ref,), total)
    for at, (grad, out) in enumerate(((grad_a, out_a), (grad_b, out_b))):
        for strip in range(strips):
            lanes = pl.ds(strip * 128, 128)
            for place, cell in enumerate(cell_order()):
                spread[strip, pl.ds(cell, tiles, stride=TH * TW), :] = total[
                    pl.ds(place * block + at * tiles, tiles), lanes
                ]
            out[:, lanes] = (grad[:, lanes].astype(jnp.float32) + spread[strip]).astype(jnp.bfloat16)


def place_half_kernel(scale, side, core_ref, half_ref, *refs):
    out, staged, done = refs[-3:]
    taps, _, width = half_ref.shape
    at = core_ref[0] if side == 0 else 1 - core_ref[0]
    lanes = pl.ds(pl.multiple_of(at * width, width), width)
    copies = []
    for tap in range(0, taps, 3):
        these = pl.ds(tap, min(3, taps - tap))
        staged[these] = half_ref[these].astype(jnp.float32) * scale
        copies.append(pltpu.make_async_copy(staged.at[these], out.at[these, :, lanes], done.at[tap]))
        copies[-1].start()
    for copy in copies:
        copy.wait()


def place_half(scale, side, core_at, half, begun=None):
    taps, group_width, width = half.shape
    specs = [pl.BlockSpec(memory_space=pltpu.SMEM)] + on_vmem(1)
    operands = [core_at, half]
    if begun is not None:
        specs.append(pl.BlockSpec(memory_space=pl.ANY))
        operands.append(begun)
    return pl.pallas_call(
        functools.partial(place_half_kernel, scale, side),
        out_shape=jax.ShapeDtypeStruct((taps, group_width, 2 * width), jnp.float32),
        in_specs=specs,
        out_specs=pl.BlockSpec(memory_space=pl.ANY),
        scratch_shapes=[
            pltpu.VMEM((taps, group_width, width), jnp.float32),
            pltpu.SemaphoreType.DMA((taps,)),
        ],
        input_output_aliases={} if begun is None else {2: 0},
        compiler_params=pltpu.CompilerParams(vmem_limit_bytes=VMEM_LIMIT),
        cost_estimate=pl.CostEstimate(flops=1000, bytes_accessed=1000, transcendentals=0),
    )(*operands)


def on_vmem(count):
    return [pl.BlockSpec(memory_space=pltpu.VMEM)] * count


def local_call(kernel, outs, scratch, flops, *operands):
    return pl.pallas_call(
        kernel,
        out_shape=tuple(outs),
        in_specs=on_vmem(len(operands)),
        out_specs=tuple(on_vmem(len(outs))),
        scratch_shapes=scratch,
        compiler_params=pltpu.CompilerParams(vmem_limit_bytes=VMEM_LIMIT),
        cost_estimate=pl.CostEstimate(flops=1000, bytes_accessed=1000, transcendentals=0),
    )(*operands)


def weights_travel(activations, upstream, routes, gate_codes, weights):
    me = lax.axis_index("expert")
    core = lax.axis_index("dp")
    inner = (me == 1) | (me == 2)
    per_device, cell_count, channels = activations.shape[1:]
    rows = per_device * cell_count
    width = channels // 2
    taps, group_width = weights.shape[2:4]
    sections = lax.axis_size("segment")

    def half(array, which):
        return lax.dynamic_slice_in_dim(array, which * width, width, array.ndim - 1)

    def near(array):
        return lax.ppermute(array, "expert", NEAR_PAIRS)

    def across(array):
        return lax.ppermute(array, ("expert", "dp"), inner_pairs())

    def from_next(array):
        return lax.ppermute(array, "segment", [((s + 1) % sections, s) for s in range(sections)])

    info = jnp.concatenate([routes[0].T, gate_codes[0].T], axis=0)
    info_b = lax.ppermute(info, "dp", SWAP)
    grad_rows = from_next(upstream[0].reshape(rows, channels))
    my_weights = half(weights[0, 0], core)
    inner_weights = across(my_weights)
    act_rows = activations[0].reshape(rows, channels)
    act_a = half(act_rows, core)
    act_b = lax.ppermute(half(act_rows, 1 - core), "dp", SWAP)
    near_weights = near(my_weights)
    grad_a = half(grad_rows, core)
    grad_b = lax.ppermute(half(grad_rows, 1 - core), "dp", SWAP)

    part = jax.ShapeDtypeStruct((taps, group_width, width), jnp.bfloat16)
    (turned,) = local_call(
        turn_kernel,
        (jax.ShapeDtypeStruct((3, width, 2 * rows), jnp.bfloat16),),
        [
            pltpu.VMEM((2 * (width // 128), rows, 128), jnp.float32),
            pltpu.VMEM((2 * rows, width), jnp.bfloat16),
        ],
        200_000_000,
        act_a, act_b,
    )
    cells, gates, far_part = local_call(
        prepare_kernel,
        (
            jax.ShapeDtypeStruct((2 * rows, width), jnp.bfloat16),
            jax.ShapeDtypeStruct((2 * per_device, 128), jnp.float32),
            part,
        ),
        [
            pltpu.VMEM((2 * (width // 128), rows, 128), jnp.float32),
            pltpu.VMEM((1, 2 * rows, width), jnp.bfloat16),
        ],
        600_000_000,
        grad_a, grad_b, turned, info, info_b,
    )
    near_weights, far_part = lax.optimization_barrier((near_weights, far_part))
    cross_weights = across(near_weights)
    first_swap = near(jnp.where(inner, inner_weights, far_part))
    scaled, mid_part, near_part, own_part = local_call(
        partial_kernel,
        (
            jax.ShapeDtypeStruct((4, 2 * rows, width), jnp.bfloat16),
            part,
            part,
            jax.ShapeDtypeStruct((taps, group_width, width), jnp.float32),
        ),
        [],
        1_200_000_000,
        cells, gates, turned,
    )
    first_swap, mid_part = lax.optimization_barrier((first_swap, mid_part))
    second_swap = near(jnp.where(inner, cross_weights, mid_part))
    far_sum = across(far_part + first_swap)
    mid_sum = across(mid_part + second_swap)
    last_swap = near(jnp.where(inner, near_part + far_sum, near_part))

    mid_weights = jnp.where(inner, inner_weights, first_swap)
    far_weights = jnp.where(inner, cross_weights, second_swap)
    (early,) = local_call(
        early_answer_kernel,
        (jax.ShapeDtypeStruct((2 * rows, width), jnp.float32),),
        [],
        1_200_000_000,
        scaled, my_weights, near_weights, mid_weights,
    )
    answer = jax.ShapeDtypeStruct((rows, width), jnp.bfloat16)
    grad_own, grad_other = local_call(
        late_answer_kernel,
        (answer, answer),
        [
            pltpu.VMEM((2 * rows, width), jnp.float32),
            pltpu.VMEM((width // 128, rows, 128), jnp.float32),
        ],
        500_000_000,
        scaled, far_weights, early, grad_a, grad_b,
    )
    grad_back = lax.ppermute(grad_other, "dp", SWAP)

    def whole(mine, other):
        return jnp.where(
            core == 0, jnp.concatenate([mine, other], axis=-1), jnp.concatenate([other, mine], axis=-1)
        )

    input_grad = whole(grad_own, grad_back).reshape(per_device, cell_count, channels)
    last_swap, input_grad = lax.optimization_barrier((last_swap, input_grad))
    kernel_sum = own_part + last_swap.astype(jnp.float32) + jnp.where(inner, mid_sum, 0).astype(jnp.float32)
    kernel_mine = kernel_sum.astype(jnp.bfloat16)
    kernel_other = lax.ppermute(kernel_mine, "dp", SWAP)
    core_at = jnp.reshape(core, (1,)).astype(jnp.int32)
    begun = place_half(1.0 / per_device, 0, core_at, kernel_mine)
    weight_grad = place_half(1.0 / per_device, 1, core_at, kernel_other, begun)
    return (input_grad[None], weight_grad[None, None])


def solution(mesh):
    placed = (
        P("segment", ("expert", "dp"), None, None),
        P("segment", ("expert", "dp"), None, None),
        P("segment", ("expert", "dp"), None),
        P("segment", ("expert", "dp"), None),
        P("segment", "expert", None, None, None),
    )
    step = weights_travel if fits_line(mesh) else body
    return jax.shard_map(
        step,
        mesh=mesh,
        in_specs=placed,
        out_specs=(
            P("segment", ("expert", "dp"), None, None),
            P("segment", "expert", None, None, None),
        ),
        check_vma=False,
    )
```

```python
import functools

import jax
import jax.numpy as jnp
import numpy as np
from jax import lax
from jax.experimental import pallas as pl
from jax.experimental.pallas import tpu as pltpu
from jax.sharding import PartitionSpec as P

TH = 4
TW = 2


def shifted(array, axis, by):
    count = lax.axis_size(axis)
    return lax.ppermute(array, axis, [(i, (i + by) % count) for i in range(count)])


def offsets_table():
    cell_count = TH * TW
    table = np.zeros((cell_count, cell_count, 9), np.float32)
    for source_cell in range(cell_count):
        for target_cell in range(cell_count):
            row_step = target_cell // TW - source_cell // TW
            col_step = target_cell % TW - source_cell % TW
            if abs(row_step) <= 1 and abs(col_step) <= 1:
                table[source_cell, target_cell, (row_step + 1) * 3 + col_step + 1] = 1.0
    return table


def by_group(rows, group_width):
    tile_count = rows.shape[0]
    cell_count = rows.shape[1]
    group_count = rows.shape[2] // group_width
    split = rows.reshape(tile_count, cell_count, group_count, group_width).transpose(2, 0, 1, 3)
    return split.reshape(group_count, tile_count, cell_count * group_width)


def transpose_conv(scaled_grads, weight):
    tile_count = scaled_grads.shape[0]
    cell_count = scaled_grads.shape[1]
    group_width = weight.shape[1]
    channels = weight.shape[2]
    group_count = channels // group_width
    selector = jnp.asarray(offsets_table(), jnp.bfloat16)
    split_weight = weight.reshape(9, group_width, group_count, group_width)
    blocks = jnp.einsum(
        "pqt,tcgo->gpoqc", selector, split_weight, preferred_element_type=jnp.float32
    )
    blocks = blocks.astype(jnp.bfloat16).reshape(
        group_count, cell_count * group_width, cell_count * group_width
    )
    grouped = by_group(scaled_grads, group_width)
    result = jnp.einsum("gnk,gkm->gnm", grouped, blocks, preferred_element_type=jnp.float32)
    result = result.reshape(group_count, tile_count, cell_count, group_width).transpose(1, 2, 0, 3)
    return result.reshape(tile_count, cell_count, channels)


def weight_corr(inputs, scaled_grads, group_width):
    cell_count = inputs.shape[1]
    channels = inputs.shape[2]
    group_count = channels // group_width
    grouped_inputs = by_group(inputs, group_width)
    grouped_grads = by_group(scaled_grads, group_width)
    moments = jnp.einsum(
        "gnk,gnm->gkm", grouped_inputs, grouped_grads, preferred_element_type=jnp.float32
    )
    moments = moments.reshape(group_count, cell_count, group_width, cell_count, group_width)
    selector = jnp.asarray(offsets_table(), jnp.float32)
    taps = jnp.einsum("gpcqo,qpt->tcgo", moments, selector, precision=lax.Precision.HIGHEST)
    return taps.reshape(9, group_width, channels)


def body(activations, upstream, routes, gate_codes, weights):
    incoming = shifted(upstream, "segment", -1)[0]
    inputs = activations[0]
    route_ids = routes[0]
    code_values = gate_codes[0].astype(jnp.float32)
    kernel = weights[0, 0]
    group_width = kernel.shape[1]
    per_device = inputs.shape[0]
    cell_count = inputs.shape[1]
    channels = inputs.shape[2]
    experts = lax.axis_size("expert")
    capacity = max(2, 4 * per_device // experts)
    gate_share = code_values / jnp.sum(code_values, axis=1, keepdims=True)
    scaled_grads = (gate_share[:, :, None, None] * incoming[:, None].astype(jnp.float32)).astype(
        jnp.bfloat16
    )
    grad_rows = scaled_grads.reshape(2 * per_device, cell_count * channels)
    input_rows = jnp.repeat(inputs, 2, axis=0).reshape(2 * per_device, cell_count * channels)
    flat_expert = route_ids.reshape(-1)
    matches = (flat_expert[:, None] == jnp.arange(experts, dtype=jnp.int32)[None, :]).astype(
        jnp.int32
    )
    earlier = jnp.cumsum(matches, axis=0) - matches
    slot_rank = jnp.sum(earlier * matches, axis=1)
    slot_place = flat_expert * capacity + slot_rank
    chooser = (
        slot_place[None, :] == jnp.arange(experts * capacity, dtype=jnp.int32)[:, None]
    ).astype(jnp.bfloat16)

    def pack_slots(rows):
        packed = jnp.dot(chooser, rows, preferred_element_type=jnp.float32).astype(jnp.bfloat16)
        return packed.reshape(experts, capacity, cell_count, channels)

    inputs_recv, grads_recv = (
        lax.all_to_all(pack_slots(input_rows), "expert", split_axis=0, concat_axis=0, tiled=True),
        lax.all_to_all(pack_slots(grad_rows), "expert", split_axis=0, concat_axis=0, tiled=True),
    )
    flat_grads = grads_recv.reshape(experts * capacity, cell_count, channels)
    answers = transpose_conv(flat_grads, kernel).astype(jnp.bfloat16)
    returned = lax.all_to_all(
        answers.reshape(experts, capacity, cell_count, channels),
        "expert",
        split_axis=0,
        concat_axis=0,
        tiled=True,
    )
    flat_inputs = inputs_recv.reshape(experts * capacity, cell_count, channels)
    local_grad = weight_corr(flat_inputs, flat_grads, group_width)
    flat_answers = returned.reshape(experts * capacity, cell_count * channels)
    per_route = jnp.dot(chooser.T, flat_answers, preferred_element_type=jnp.float32).reshape(
        per_device, 2, cell_count, channels
    )
    input_grad = (incoming.astype(jnp.float32) + per_route[:, 0] + per_route[:, 1]).astype(
        jnp.bfloat16
    )
    total_grad = lax.psum(local_grad, "dp") / per_device
    return (input_grad[None], total_grad[None, None])


LINE = 4
CORES = 2
NEAR_PAIRS = [(0, 1), (1, 0), (2, 3), (3, 2)]
SWAP = [(0, 1), (1, 0)]
VMEM_LIMIT = 16 * 1024 * 1024


def inner_pairs():
    crossing = {1: 2, 2: 1}
    pairs = []
    for e in range(LINE):
        for d in range(CORES):
            target = (crossing[e], d) if e in crossing else (e, 1 - d)
            pairs.append((CORES * e + d, CORES * target[0] + target[1]))
    return pairs


def fits_line(mesh):
    return mesh.shape["expert"] == LINE and mesh.shape["dp"] == CORES


def cell_order():
    return [row * TW + col for col in range(TW) for row in range(TH)]


def own_gates(info, expert):
    codes = info[2:4].astype(jnp.float32)
    hits = jnp.where(info[0:2] == expert, codes, 0.0)
    return (hits[0:1] + hits[1:2]) / (codes[0:1] + codes[1:2])


def gate_columns(info_ref, experts):
    rows = [own_gates(info_ref[...], expert) for expert in experts]
    count = rows[0].shape[1]
    table = jnp.concatenate(rows + [jnp.zeros((128 - len(rows), count), jnp.float32)], axis=0)
    table = jnp.concatenate([table, jnp.zeros((128, 128 - count), jnp.float32)], axis=1)
    return table.T[:count]


def slot_experts():
    me = lax.axis_index("expert")
    outer = (me == 0) | (me == 3)
    mid = jnp.where(outer, 2, 3)
    far = 5 - mid
    return [me, me ^ 1, me ^ mid, me ^ far]


def rows_by_cell(refs, wide):
    strips = refs[0].shape[1] // 128
    tiles = refs[0].shape[0] // (TH * TW)
    for at, ref in enumerate(refs):
        for strip in range(strips):
            wide[at * strips + strip] = ref[:, pl.ds(strip * 128, 128)].astype(jnp.float32)

    def cell_rows(at, cell):
        pieces = [wide[at * strips + strip, pl.ds(cell, tiles, stride=TH * TW), :] for strip in range(strips)]
        return jnp.concatenate(pieces, axis=1)

    return cell_rows


def turn_kernel(act_a, act_b, turned, wide, cells):
    width = act_a.shape[1]
    block = 2 * act_a.shape[0] // (TH * TW)
    column = TH * block
    cell_rows = rows_by_cell((act_a, act_b), wide)
    for place, cell in enumerate(cell_order()):
        act_rows = jnp.concatenate([cell_rows(0, cell), cell_rows(1, cell)], axis=0)
        cells[pl.ds(place * block, block), :] = act_rows.astype(jnp.bfloat16)
    empty = jnp.zeros((block, width), jnp.bfloat16)
    for col in range(TW):
        rows = cells[pl.ds(col * column, column), :]
        turned[1, :, pl.ds(col * column, column)] = rows.T
        turned[2, :, pl.ds(col * column, column)] = jnp.concatenate([rows[block:], empty], axis=0).T
        turned[0, :, pl.ds(col * column, column)] = jnp.concatenate([empty, rows[:-block]], axis=0).T


def prepare_kernel(grad_a, grad_b, turned, info_a, info_b, cells, gates, far_ref, wide, scaled):
    tiles = info_a.shape[1]
    block = 2 * tiles
    cell_rows = rows_by_cell((grad_a, grad_b), wide)
    experts = slot_experts()
    gates[pl.ds(0, tiles), :] = gate_columns(info_a, experts)
    gates[pl.ds(tiles, tiles), :] = gate_columns(info_b, experts)
    far_gate = gates[:, 3:4]
    for place, cell in enumerate(cell_order()):
        both = jnp.concatenate([cell_rows(0, cell), cell_rows(1, cell)], axis=0)
        cells[pl.ds(place * block, block), :] = both.astype(jnp.bfloat16)
        scaled[0, pl.ds(place * block, block), :] = (both * far_gate).astype(jnp.bfloat16)
    kernel_gradient(turned, scaled, 0, far_ref)


def kernel_gradient(turned, scaled_ref, slot, ref):
    width, column = turned.shape[1], turned.shape[2] // TW
    low_half = lax.broadcasted_iota(jnp.int32, (64, 128), 1) < 64
    for row_off in (-1, 0, 1):
        for col_off in (-1, 0, 1):
            lhs = turned[row_off + 1]
            rhs = scaled_ref[slot]
            if col_off == 1:
                lhs, rhs = lhs[:, column:], rhs[:column]
            if col_off == -1:
                lhs, rhs = lhs[:, :column], rhs[column:]
            full = jnp.dot(lhs, rhs, preferred_element_type=jnp.float32)
            tap = (row_off + 1) * 3 + col_off + 1
            for pair in range(width // 128):
                base = pair * 128
                piece = jnp.where(
                    low_half,
                    full[base : base + 64, base : base + 128],
                    full[base + 64 : base + 128, base : base + 128],
                )
                ref[tap, :, pl.ds(base, 128)] = piece.astype(ref.dtype)


def partial_kernel(cells, gates, turned, scaled_ref, mid_ref, near_ref, own_ref):
    block = gates.shape[0]
    for place in range(TH * TW):
        rows = cells[pl.ds(place * block, block), :].astype(jnp.float32)
        for slot in range(4):
            scaled_ref[slot, pl.ds(place * block, block), :] = (rows * gates[:, slot : slot + 1]).astype(jnp.bfloat16)
    for slot, ref in ((2, mid_ref), (1, near_ref), (0, own_ref)):
        kernel_gradient(turned, scaled_ref, slot, ref)


def add_answers(scaled_ref, slots, kernels, total):
    width = total.shape[1]
    block = total.shape[0] // (TH * TW)
    lane_group = lax.broadcasted_iota(jnp.int32, (64, width), 1) // 64
    masks = [jnp.where(lane_group == g, 1.0, 0.0).astype(jnp.bfloat16) for g in range(width // 64)]
    for slot, ref in zip(slots, kernels):
        for row_off in (-1, 0, 1):
            for col_off in (-1, 0, 1):
                tap = (row_off + 1) * 3 + col_off + 1
                kernel = ref[tap]
                blocks = jnp.concatenate([kernel * mask for mask in masks], axis=0)
                first = max(0, -row_off)
                rows = (TH - abs(row_off)) * block
                for col in range(TW):
                    if not 0 <= col + col_off < TW:
                        continue
                    source = (col * TH + first) * block
                    target = ((col + col_off) * TH + first + row_off) * block
                    total[pl.ds(target, rows), :] += lax.dot_general(
                        scaled_ref[slot, pl.ds(source, rows), :],
                        blocks,
                        (((1,), (1,)), ((), ())),
                        preferred_element_type=jnp.float32,
                    )


def early_answer_kernel(scaled_ref, own_ref, near_ref, mid_ref, total):
    total[...] = jnp.zeros_like(total)
    add_answers(scaled_ref, (0, 1, 2), (own_ref, near_ref, mid_ref), total)


def late_answer_kernel(scaled_ref, far_ref, early, grad_a, grad_b, out_a, out_b, total, spread):
    tiles = grad_a.shape[0] // (TH * TW)
    block = 2 * tiles
    strips = grad_a.shape[1] // 128
    total[...] = early[...]
    add_answers(scaled_ref, (3,), (far_ref,), total)
    for at, (grad, out) in enumerate(((grad_a, out_a), (grad_b, out_b))):
        for strip in range(strips):
            lanes = pl.ds(strip * 128, 128)
            for place, cell in enumerate(cell_order()):
                spread[strip, pl.ds(cell, tiles, stride=TH * TW), :] = total[
                    pl.ds(place * block + at * tiles, tiles), lanes
                ]
            out[:, lanes] = (grad[:, lanes].astype(jnp.float32) + spread[strip]).astype(jnp.bfloat16)


def place_half_kernel(scale, side, core_ref, half_ref, *refs):
    out, staged, done = refs[-3:]
    taps, _, width = half_ref.shape
    at = core_ref[0] if side == 0 else 1 - core_ref[0]
    lanes = pl.ds(pl.multiple_of(at * width, width), width)
    copies = []
    for tap in range(0, taps, 3):
        these = pl.ds(tap, min(3, taps - tap))
        staged[these] = half_ref[these].astype(jnp.float32) * scale
        copies.append(pltpu.make_async_copy(staged.at[these], out.at[these, :, lanes], done.at[tap]))
        copies[-1].start()
    for copy in copies:
        copy.wait()


def place_half(scale, side, core_at, half, begun=None):
    taps, group_width, width = half.shape
    specs = [pl.BlockSpec(memory_space=pltpu.SMEM)] + on_vmem(1)
    operands = [core_at, half]
    if begun is not None:
        specs.append(pl.BlockSpec(memory_space=pl.ANY))
        operands.append(begun)
    return pl.pallas_call(
        functools.partial(place_half_kernel, scale, side),
        out_shape=jax.ShapeDtypeStruct((taps, group_width, 2 * width), jnp.float32),
        in_specs=specs,
        out_specs=pl.BlockSpec(memory_space=pl.ANY),
        scratch_shapes=[
            pltpu.VMEM((taps, group_width, width), jnp.float32),
            pltpu.SemaphoreType.DMA((taps,)),
        ],
        input_output_aliases={} if begun is None else {2: 0},
        compiler_params=pltpu.CompilerParams(vmem_limit_bytes=VMEM_LIMIT),
        cost_estimate=pl.CostEstimate(flops=1000, bytes_accessed=600_000, transcendentals=0),
    )(*operands)


def on_vmem(count):
    return [pl.BlockSpec(memory_space=pltpu.VMEM)] * count


def local_call(kernel, outs, scratch, flops, *operands):
    return pl.pallas_call(
        kernel,
        out_shape=tuple(outs),
        in_specs=on_vmem(len(operands)),
        out_specs=tuple(on_vmem(len(outs))),
        scratch_shapes=scratch,
        compiler_params=pltpu.CompilerParams(vmem_limit_bytes=VMEM_LIMIT),
        cost_estimate=pl.CostEstimate(flops=flops, bytes_accessed=1000, transcendentals=0),
    )(*operands)


def copy_kernel(source, out):
    out[...] = source[...]


def weights_travel(activations, upstream, routes, gate_codes, weights):
    me = lax.axis_index("expert")
    core = lax.axis_index("dp")
    inner = (me == 1) | (me == 2)
    per_device, cell_count, channels = activations.shape[1:]
    rows = per_device * cell_count
    width = channels // 2
    taps, group_width = weights.shape[2:4]
    sections = lax.axis_size("segment")

    def half(array, which):
        return lax.dynamic_slice_in_dim(array, which * width, width, array.ndim - 1)

    def near(array):
        return lax.ppermute(array, "expert", NEAR_PAIRS)

    def across(array):
        return lax.ppermute(array, ("expert", "dp"), inner_pairs())

    def from_next(array):
        return lax.ppermute(array, "segment", [((s + 1) % sections, s) for s in range(sections)])

    info = jnp.concatenate([routes[0].T, gate_codes[0].T], axis=0)
    info_b = lax.ppermute(info, "dp", SWAP)
    grad_rows = from_next(upstream[0].reshape(rows, channels))
    my_weights = half(weights[0, 0], core)
    inner_weights = across(my_weights)
    (inner_weights,) = local_call(
        copy_kernel,
        (jax.ShapeDtypeStruct(inner_weights.shape, inner_weights.dtype),),
        [],
        20_000_000_000,
        inner_weights,
    )
    act_rows = activations[0].reshape(rows, channels)
    act_a = half(act_rows, core)
    act_b = lax.ppermute(half(act_rows, 1 - core), "dp", SWAP)
    near_weights = near(my_weights)
    grad_a = half(grad_rows, core)
    grad_b = lax.ppermute(half(grad_rows, 1 - core), "dp", SWAP)

    part = jax.ShapeDtypeStruct((taps, group_width, width), jnp.bfloat16)
    (turned,) = local_call(
        turn_kernel,
        (jax.ShapeDtypeStruct((3, width, 2 * rows), jnp.bfloat16),),
        [
            pltpu.VMEM((2 * (width // 128), rows, 128), jnp.float32),
            pltpu.VMEM((2 * rows, width), jnp.bfloat16),
        ],
        200_000_000,
        act_a, act_b,
    )
    cells, gates, far_part = local_call(
        prepare_kernel,
        (
            jax.ShapeDtypeStruct((2 * rows, width), jnp.bfloat16),
            jax.ShapeDtypeStruct((2 * per_device, 128), jnp.float32),
            part,
        ),
        [
            pltpu.VMEM((2 * (width // 128), rows, 128), jnp.float32),
            pltpu.VMEM((1, 2 * rows, width), jnp.bfloat16),
        ],
        600_000_000,
        grad_a, grad_b, turned, info, info_b,
    )
    cross_weights = across(near_weights)
    first_swap = near(jnp.where(inner, inner_weights, far_part))
    scaled, mid_part, near_part, own_part = local_call(
        partial_kernel,
        (
            jax.ShapeDtypeStruct((4, 2 * rows, width), jnp.bfloat16),
            part,
            part,
            jax.ShapeDtypeStruct((taps, group_width, width), jnp.float32),
        ),
        [],
        1_200_000_000,
        cells, gates, turned,
    )
    first_swap, mid_part = lax.optimization_barrier((first_swap, mid_part))
    second_swap = near(jnp.where(inner, cross_weights, mid_part))
    far_sum = across(far_part + first_swap)
    mid_sum = across(mid_part + second_swap)
    last_swap = near(jnp.where(inner, near_part + far_sum, near_part))

    mid_weights = jnp.where(inner, inner_weights, first_swap)
    far_weights = jnp.where(inner, cross_weights, second_swap)
    (early,) = local_call(
        early_answer_kernel,
        (jax.ShapeDtypeStruct((2 * rows, width), jnp.float32),),
        [],
        1_200_000_000,
        scaled, my_weights, near_weights, mid_weights,
    )
    answer = jax.ShapeDtypeStruct((rows, width), jnp.bfloat16)
    grad_own, grad_other = local_call(
        late_answer_kernel,
        (answer, answer),
        [
            pltpu.VMEM((2 * rows, width), jnp.float32),
            pltpu.VMEM((width // 128, rows, 128), jnp.float32),
        ],
        500_000_000,
        scaled, far_weights, early, grad_a, grad_b,
    )
    grad_back = lax.ppermute(grad_other, "dp", SWAP)

    def whole(mine, other):
        return jnp.where(
            core == 0, jnp.concatenate([mine, other], axis=-1), jnp.concatenate([other, mine], axis=-1)
        )

    input_grad = whole(grad_own, grad_back).reshape(per_device, cell_count, channels)
    last_swap, input_grad = lax.optimization_barrier((last_swap, input_grad))
    kernel_sum = own_part + last_swap.astype(jnp.float32) + jnp.where(inner, mid_sum, 0).astype(jnp.float32)
    kernel_mine = kernel_sum.astype(jnp.bfloat16)
    kernel_other = lax.ppermute(kernel_mine, "dp", SWAP)
    core_at = jnp.reshape(core, (1,)).astype(jnp.int32)
    begun = place_half(1.0 / per_device, 0, core_at, kernel_mine)
    weight_grad = place_half(1.0 / per_device, 1, core_at, kernel_other, begun)
    return (input_grad[None], weight_grad[None, None])


def solution(mesh):
    placed = (
        P("segment", ("expert", "dp"), None, None),
        P("segment", ("expert", "dp"), None, None),
        P("segment", ("expert", "dp"), None),
        P("segment", ("expert", "dp"), None),
        P("segment", "expert", None, None, None),
    )
    step = weights_travel if fits_line(mesh) else body
    return jax.shard_map(
        step,
        mesh=mesh,
        in_specs=placed,
        out_specs=(
            P("segment", ("expert", "dp"), None, None),
            P("segment", "expert", None, None, None),
        ),
        check_vma=False,
    )
```

```python
import functools

import jax
import jax.numpy as jnp
import numpy as np
from jax import lax
from jax.experimental import pallas as pl
from jax.experimental.pallas import tpu as pltpu
from jax.sharding import PartitionSpec as P

TH = 4
TW = 2


def shifted(array, axis, by):
    count = lax.axis_size(axis)
    return lax.ppermute(array, axis, [(i, (i + by) % count) for i in range(count)])


def offsets_table():
    cell_count = TH * TW
    table = np.zeros((cell_count, cell_count, 9), np.float32)
    for source_cell in range(cell_count):
        for target_cell in range(cell_count):
            row_step = target_cell // TW - source_cell // TW
            col_step = target_cell % TW - source_cell % TW
            if abs(row_step) <= 1 and abs(col_step) <= 1:
                table[source_cell, target_cell, (row_step + 1) * 3 + col_step + 1] = 1.0
    return table


def by_group(rows, group_width):
    tile_count = rows.shape[0]
    cell_count = rows.shape[1]
    group_count = rows.shape[2] // group_width
    split = rows.reshape(tile_count, cell_count, group_count, group_width).transpose(2, 0, 1, 3)
    return split.reshape(group_count, tile_count, cell_count * group_width)


def transpose_conv(scaled_grads, weight):
    tile_count = scaled_grads.shape[0]
    cell_count = scaled_grads.shape[1]
    group_width = weight.shape[1]
    channels = weight.shape[2]
    group_count = channels // group_width
    selector = jnp.asarray(offsets_table(), jnp.bfloat16)
    split_weight = weight.reshape(9, group_width, group_count, group_width)
    blocks = jnp.einsum(
        "pqt,tcgo->gpoqc", selector, split_weight, preferred_element_type=jnp.float32
    )
    blocks = blocks.astype(jnp.bfloat16).reshape(
        group_count, cell_count * group_width, cell_count * group_width
    )
    grouped = by_group(scaled_grads, group_width)
    result = jnp.einsum("gnk,gkm->gnm", grouped, blocks, preferred_element_type=jnp.float32)
    result = result.reshape(group_count, tile_count, cell_count, group_width).transpose(1, 2, 0, 3)
    return result.reshape(tile_count, cell_count, channels)


def weight_corr(inputs, scaled_grads, group_width):
    cell_count = inputs.shape[1]
    channels = inputs.shape[2]
    group_count = channels // group_width
    grouped_inputs = by_group(inputs, group_width)
    grouped_grads = by_group(scaled_grads, group_width)
    moments = jnp.einsum(
        "gnk,gnm->gkm", grouped_inputs, grouped_grads, preferred_element_type=jnp.float32
    )
    moments = moments.reshape(group_count, cell_count, group_width, cell_count, group_width)
    selector = jnp.asarray(offsets_table(), jnp.float32)
    taps = jnp.einsum("gpcqo,qpt->tcgo", moments, selector, precision=lax.Precision.HIGHEST)
    return taps.reshape(9, group_width, channels)


def body(activations, upstream, routes, gate_codes, weights):
    incoming = shifted(upstream, "segment", -1)[0]
    inputs = activations[0]
    route_ids = routes[0]
    code_values = gate_codes[0].astype(jnp.float32)
    kernel = weights[0, 0]
    group_width = kernel.shape[1]
    per_device = inputs.shape[0]
    cell_count = inputs.shape[1]
    channels = inputs.shape[2]
    experts = lax.axis_size("expert")
    capacity = max(2, 4 * per_device // experts)
    gate_share = code_values / jnp.sum(code_values, axis=1, keepdims=True)
    scaled_grads = (gate_share[:, :, None, None] * incoming[:, None].astype(jnp.float32)).astype(
        jnp.bfloat16
    )
    grad_rows = scaled_grads.reshape(2 * per_device, cell_count * channels)
    input_rows = jnp.repeat(inputs, 2, axis=0).reshape(2 * per_device, cell_count * channels)
    flat_expert = route_ids.reshape(-1)
    matches = (flat_expert[:, None] == jnp.arange(experts, dtype=jnp.int32)[None, :]).astype(
        jnp.int32
    )
    earlier = jnp.cumsum(matches, axis=0) - matches
    slot_rank = jnp.sum(earlier * matches, axis=1)
    slot_place = flat_expert * capacity + slot_rank
    chooser = (
        slot_place[None, :] == jnp.arange(experts * capacity, dtype=jnp.int32)[:, None]
    ).astype(jnp.bfloat16)

    def pack_slots(rows):
        packed = jnp.dot(chooser, rows, preferred_element_type=jnp.float32).astype(jnp.bfloat16)
        return packed.reshape(experts, capacity, cell_count, channels)

    inputs_recv, grads_recv = (
        lax.all_to_all(pack_slots(input_rows), "expert", split_axis=0, concat_axis=0, tiled=True),
        lax.all_to_all(pack_slots(grad_rows), "expert", split_axis=0, concat_axis=0, tiled=True),
    )
    flat_grads = grads_recv.reshape(experts * capacity, cell_count, channels)
    answers = transpose_conv(flat_grads, kernel).astype(jnp.bfloat16)
    returned = lax.all_to_all(
        answers.reshape(experts, capacity, cell_count, channels),
        "expert",
        split_axis=0,
        concat_axis=0,
        tiled=True,
    )
    flat_inputs = inputs_recv.reshape(experts * capacity, cell_count, channels)
    local_grad = weight_corr(flat_inputs, flat_grads, group_width)
    flat_answers = returned.reshape(experts * capacity, cell_count * channels)
    per_route = jnp.dot(chooser.T, flat_answers, preferred_element_type=jnp.float32).reshape(
        per_device, 2, cell_count, channels
    )
    input_grad = (incoming.astype(jnp.float32) + per_route[:, 0] + per_route[:, 1]).astype(
        jnp.bfloat16
    )
    total_grad = lax.psum(local_grad, "dp") / per_device
    return (input_grad[None], total_grad[None, None])


LINE = 4
CORES = 2
NEAR_PAIRS = [(0, 1), (1, 0), (2, 3), (3, 2)]
SWAP = [(0, 1), (1, 0)]
VMEM_LIMIT = 16 * 1024 * 1024


def inner_pairs():
    crossing = {1: 2, 2: 1}
    pairs = []
    for e in range(LINE):
        for d in range(CORES):
            target = (crossing[e], d) if e in crossing else (e, 1 - d)
            pairs.append((CORES * e + d, CORES * target[0] + target[1]))
    return pairs


def fits_line(mesh):
    return mesh.shape["expert"] == LINE and mesh.shape["dp"] == CORES


def cell_order():
    return [row * TW + col for col in range(TW) for row in range(TH)]


def own_gates(info, expert):
    codes = info[2:4].astype(jnp.float32)
    hits = jnp.where(info[0:2] == expert, codes, 0.0)
    return (hits[0:1] + hits[1:2]) / (codes[0:1] + codes[1:2])


def gate_columns(info_ref, experts):
    rows = [own_gates(info_ref[...], expert) for expert in experts]
    count = rows[0].shape[1]
    table = jnp.concatenate(rows + [jnp.zeros((128 - len(rows), count), jnp.float32)], axis=0)
    table = jnp.concatenate([table, jnp.zeros((128, 128 - count), jnp.float32)], axis=1)
    return table.T[:count]


def slot_experts():
    me = lax.axis_index("expert")
    outer = (me == 0) | (me == 3)
    mid = jnp.where(outer, 2, 3)
    far = 5 - mid
    return [me, me ^ 1, me ^ mid, me ^ far]


def rows_by_cell(refs, wide):
    strips = refs[0].shape[1] // 128
    tiles = refs[0].shape[0] // (TH * TW)
    for at, ref in enumerate(refs):
        for strip in range(strips):
            wide[at * strips + strip] = ref[:, pl.ds(strip * 128, 128)].astype(jnp.float32)

    def cell_rows(at, cell):
        pieces = [wide[at * strips + strip, pl.ds(cell, tiles, stride=TH * TW), :] for strip in range(strips)]
        return jnp.concatenate(pieces, axis=1)

    return cell_rows


def turn_kernel(act_a, act_b, turned, wide, cells):
    width = act_a.shape[1]
    block = 2 * act_a.shape[0] // (TH * TW)
    column = TH * block
    cell_rows = rows_by_cell((act_a, act_b), wide)
    for place, cell in enumerate(cell_order()):
        act_rows = jnp.concatenate([cell_rows(0, cell), cell_rows(1, cell)], axis=0)
        cells[pl.ds(place * block, block), :] = act_rows.astype(jnp.bfloat16)
    empty = jnp.zeros((block, width), jnp.bfloat16)
    for col in range(TW):
        rows = cells[pl.ds(col * column, column), :]
        turned[1, :, pl.ds(col * column, column)] = rows.T
        turned[2, :, pl.ds(col * column, column)] = jnp.concatenate([rows[block:], empty], axis=0).T
        turned[0, :, pl.ds(col * column, column)] = jnp.concatenate([empty, rows[:-block]], axis=0).T


def prepare_kernel(grad_a, grad_b, turned, info_a, info_b, cells, gates, far_ref, wide, scaled):
    tiles = info_a.shape[1]
    block = 2 * tiles
    cell_rows = rows_by_cell((grad_a, grad_b), wide)
    experts = slot_experts()
    gates[pl.ds(0, tiles), :] = gate_columns(info_a, experts)
    gates[pl.ds(tiles, tiles), :] = gate_columns(info_b, experts)
    far_gate = gates[:, 3:4]
    for place, cell in enumerate(cell_order()):
        both = jnp.concatenate([cell_rows(0, cell), cell_rows(1, cell)], axis=0)
        cells[pl.ds(place * block, block), :] = both.astype(jnp.bfloat16)
        scaled[0, pl.ds(place * block, block), :] = (both * far_gate).astype(jnp.bfloat16)
    kernel_gradient(turned, scaled, 0, far_ref)


def kernel_gradient(turned, scaled_ref, slot, ref):
    width, column = turned.shape[1], turned.shape[2] // TW
    low_half = lax.broadcasted_iota(jnp.int32, (64, 128), 1) < 64
    for row_off in (-1, 0, 1):
        for col_off in (-1, 0, 1):
            lhs = turned[row_off + 1]
            rhs = scaled_ref[slot]
            if col_off == 1:
                lhs, rhs = lhs[:, column:], rhs[:column]
            if col_off == -1:
                lhs, rhs = lhs[:, :column], rhs[column:]
            full = jnp.dot(lhs, rhs, preferred_element_type=jnp.float32)
            tap = (row_off + 1) * 3 + col_off + 1
            for pair in range(width // 128):
                base = pair * 128
                piece = jnp.where(
                    low_half,
                    full[base : base + 64, base : base + 128],
                    full[base + 64 : base + 128, base : base + 128],
                )
                ref[tap, :, pl.ds(base, 128)] = piece.astype(ref.dtype)


def partial_kernel(cells, gates, turned, scaled_ref, mid_ref, near_ref, own_ref):
    block = gates.shape[0]
    for place in range(TH * TW):
        rows = cells[pl.ds(place * block, block), :].astype(jnp.float32)
        for slot in range(4):
            scaled_ref[slot, pl.ds(place * block, block), :] = (rows * gates[:, slot : slot + 1]).astype(jnp.bfloat16)
    for slot, ref in ((2, mid_ref), (1, near_ref), (0, own_ref)):
        kernel_gradient(turned, scaled_ref, slot, ref)


def add_answers(scaled_ref, slots, kernels, total):
    width = total.shape[1]
    block = total.shape[0] // (TH * TW)
    lane_group = lax.broadcasted_iota(jnp.int32, (64, width), 1) // 64
    masks = [jnp.where(lane_group == g, 1.0, 0.0).astype(jnp.bfloat16) for g in range(width // 64)]
    for slot, ref in zip(slots, kernels):
        for row_off in (-1, 0, 1):
            for col_off in (-1, 0, 1):
                tap = (row_off + 1) * 3 + col_off + 1
                kernel = ref[tap]
                blocks = jnp.concatenate([kernel * mask for mask in masks], axis=0)
                first = max(0, -row_off)
                rows = (TH - abs(row_off)) * block
                for col in range(TW):
                    if not 0 <= col + col_off < TW:
                        continue
                    source = (col * TH + first) * block
                    target = ((col + col_off) * TH + first + row_off) * block
                    total[pl.ds(target, rows), :] += lax.dot_general(
                        scaled_ref[slot, pl.ds(source, rows), :],
                        blocks,
                        (((1,), (1,)), ((), ())),
                        preferred_element_type=jnp.float32,
                    )


def early_answer_kernel(scaled_ref, own_ref, near_ref, total):
    total[...] = jnp.zeros_like(total)
    add_answers(scaled_ref, (0, 1), (own_ref, near_ref), total)


def late_answer_kernel(scaled_ref, mid_ref, far_ref, early, grad_a, grad_b, out_a, out_b, total, spread):
    tiles = grad_a.shape[0] // (TH * TW)
    block = 2 * tiles
    strips = grad_a.shape[1] // 128
    total[...] = early[...]
    add_answers(scaled_ref, (2, 3), (mid_ref, far_ref), total)
    for at, (grad, out) in enumerate(((grad_a, out_a), (grad_b, out_b))):
        for strip in range(strips):
            lanes = pl.ds(strip * 128, 128)
            for place, cell in enumerate(cell_order()):
                spread[strip, pl.ds(cell, tiles, stride=TH * TW), :] = total[
                    pl.ds(place * block + at * tiles, tiles), lanes
                ]
            out[:, lanes] = (grad[:, lanes].astype(jnp.float32) + spread[strip]).astype(jnp.bfloat16)


def place_half_kernel(scale, side, core_ref, half_ref, *refs):
    out, staged, done = refs[-3:]
    taps, _, width = half_ref.shape
    at = core_ref[0] if side == 0 else 1 - core_ref[0]
    lanes = pl.ds(pl.multiple_of(at * width, width), width)
    copies = []
    for tap in range(0, taps, 3):
        these = pl.ds(tap, min(3, taps - tap))
        staged[these] = half_ref[these].astype(jnp.float32) * scale
        copies.append(pltpu.make_async_copy(staged.at[these], out.at[these, :, lanes], done.at[tap]))
        copies[-1].start()
    for copy in copies:
        copy.wait()


def place_half(scale, side, core_at, half, begun=None):
    taps, group_width, width = half.shape
    specs = [pl.BlockSpec(memory_space=pltpu.SMEM)] + on_vmem(1)
    operands = [core_at, half]
    if begun is not None:
        specs.append(pl.BlockSpec(memory_space=pl.ANY))
        operands.append(begun)
    return pl.pallas_call(
        functools.partial(place_half_kernel, scale, side),
        out_shape=jax.ShapeDtypeStruct((taps, group_width, 2 * width), jnp.float32),
        in_specs=specs,
        out_specs=pl.BlockSpec(memory_space=pl.ANY),
        scratch_shapes=[
            pltpu.VMEM((taps, group_width, width), jnp.float32),
            pltpu.SemaphoreType.DMA((taps,)),
        ],
        input_output_aliases={} if begun is None else {2: 0},
        compiler_params=pltpu.CompilerParams(vmem_limit_bytes=VMEM_LIMIT),
        cost_estimate=pl.CostEstimate(flops=1000, bytes_accessed=600_000, transcendentals=0),
    )(*operands)


def on_vmem(count):
    return [pl.BlockSpec(memory_space=pltpu.VMEM)] * count


def local_call(kernel, outs, scratch, flops, *operands):
    return pl.pallas_call(
        kernel,
        out_shape=tuple(outs),
        in_specs=on_vmem(len(operands)),
        out_specs=tuple(on_vmem(len(outs))),
        scratch_shapes=scratch,
        compiler_params=pltpu.CompilerParams(vmem_limit_bytes=VMEM_LIMIT),
        cost_estimate=pl.CostEstimate(flops=flops, bytes_accessed=1000, transcendentals=0),
    )(*operands)


def copy_kernel(source, out):
    out[...] = source[...]


def weights_travel(activations, upstream, routes, gate_codes, weights):
    me = lax.axis_index("expert")
    core = lax.axis_index("dp")
    inner = (me == 1) | (me == 2)
    per_device, cell_count, channels = activations.shape[1:]
    rows = per_device * cell_count
    width = channels // 2
    taps, group_width = weights.shape[2:4]
    sections = lax.axis_size("segment")

    def half(array, which):
        return lax.dynamic_slice_in_dim(array, which * width, width, array.ndim - 1)

    def near(array):
        return lax.ppermute(array, "expert", NEAR_PAIRS)

    def across(array):
        return lax.ppermute(array, ("expert", "dp"), inner_pairs())

    def from_next(array):
        return lax.ppermute(array, "segment", [((s + 1) % sections, s) for s in range(sections)])

    info = jnp.concatenate([routes[0].T, gate_codes[0].T], axis=0)
    info_b = lax.ppermute(info, "dp", SWAP)
    grad_rows = from_next(upstream[0].reshape(rows, channels))
    my_weights = half(weights[0, 0], core)
    inner_weights = across(my_weights)
    (inner_weights,) = local_call(
        copy_kernel,
        (jax.ShapeDtypeStruct(inner_weights.shape, inner_weights.dtype),),
        [],
        20_000_000_000,
        inner_weights,
    )
    act_rows = activations[0].reshape(rows, channels)
    act_a = half(act_rows, core)
    act_b = lax.ppermute(half(act_rows, 1 - core), "dp", SWAP)
    near_weights = near(my_weights)
    grad_a = half(grad_rows, core)
    grad_b = lax.ppermute(half(grad_rows, 1 - core), "dp", SWAP)

    part = jax.ShapeDtypeStruct((taps, group_width, width), jnp.bfloat16)
    (turned,) = local_call(
        turn_kernel,
        (jax.ShapeDtypeStruct((3, width, 2 * rows), jnp.bfloat16),),
        [
            pltpu.VMEM((2 * (width // 128), rows, 128), jnp.float32),
            pltpu.VMEM((2 * rows, width), jnp.bfloat16),
        ],
        200_000_000,
        act_a, act_b,
    )
    cells, gates, far_part = local_call(
        prepare_kernel,
        (
            jax.ShapeDtypeStruct((2 * rows, width), jnp.bfloat16),
            jax.ShapeDtypeStruct((2 * per_device, 128), jnp.float32),
            part,
        ),
        [
            pltpu.VMEM((2 * (width // 128), rows, 128), jnp.float32),
            pltpu.VMEM((1, 2 * rows, width), jnp.bfloat16),
        ],
        600_000_000,
        grad_a, grad_b, turned, info, info_b,
    )
    cross_weights = across(near_weights)
    first_swap = near(jnp.where(inner, inner_weights, far_part))
    scaled, mid_part, near_part, own_part = local_call(
        partial_kernel,
        (
            jax.ShapeDtypeStruct((4, 2 * rows, width), jnp.bfloat16),
            part,
            part,
            jax.ShapeDtypeStruct((taps, group_width, width), jnp.float32),
        ),
        [],
        1_200_000_000,
        cells, gates, turned,
    )
    first_swap, mid_part = lax.optimization_barrier((first_swap, mid_part))
    second_swap = near(jnp.where(inner, cross_weights, mid_part))
    far_sum = across(far_part + first_swap)
    mid_sum = across(mid_part + second_swap)
    last_swap = near(jnp.where(inner, near_part + far_sum, near_part))

    mid_weights = jnp.where(inner, inner_weights, first_swap)
    far_weights = jnp.where(inner, cross_weights, second_swap)
    (early,) = local_call(
        early_answer_kernel,
        (jax.ShapeDtypeStruct((2 * rows, width), jnp.float32),),
        [],
        1_200_000_000,
        scaled, my_weights, near_weights,
    )
    answer = jax.ShapeDtypeStruct((rows, width), jnp.bfloat16)
    grad_own, grad_other = local_call(
        late_answer_kernel,
        (answer, answer),
        [
            pltpu.VMEM((2 * rows, width), jnp.float32),
            pltpu.VMEM((width // 128, rows, 128), jnp.float32),
        ],
        500_000_000,
        scaled, mid_weights, far_weights, early, grad_a, grad_b,
    )
    grad_back = lax.ppermute(grad_other, "dp", SWAP)

    def whole(mine, other):
        return jnp.where(
            core == 0, jnp.concatenate([mine, other], axis=-1), jnp.concatenate([other, mine], axis=-1)
        )

    input_grad = whole(grad_own, grad_back).reshape(per_device, cell_count, channels)
    last_swap, input_grad = lax.optimization_barrier((last_swap, input_grad))
    kernel_sum = own_part + last_swap.astype(jnp.float32) + jnp.where(inner, mid_sum, 0).astype(jnp.float32)
    kernel_mine = kernel_sum.astype(jnp.bfloat16)
    kernel_other = lax.ppermute(kernel_mine, "dp", SWAP)
    core_at = jnp.reshape(core, (1,)).astype(jnp.int32)
    begun = place_half(1.0 / per_device, 0, core_at, kernel_mine)
    weight_grad = place_half(1.0 / per_device, 1, core_at, kernel_other, begun)
    return (input_grad[None], weight_grad[None, None])


def solution(mesh):
    placed = (
        P("segment", ("expert", "dp"), None, None),
        P("segment", ("expert", "dp"), None, None),
        P("segment", ("expert", "dp"), None),
        P("segment", ("expert", "dp"), None),
        P("segment", "expert", None, None, None),
    )
    step = weights_travel if fits_line(mesh) else body
    return jax.shard_map(
        step,
        mesh=mesh,
        in_specs=placed,
        out_specs=(
            P("segment", ("expert", "dp"), None, None),
            P("segment", "expert", None, None, None),
        ),
        check_vma=False,
    )
```

```python
import functools

import jax
import jax.numpy as jnp
import numpy as np
from jax import lax
from jax.experimental import pallas as pl
from jax.experimental.pallas import tpu as pltpu
from jax.sharding import PartitionSpec as P

TH = 4
TW = 2


def shifted(array, axis, by):
    count = lax.axis_size(axis)
    return lax.ppermute(array, axis, [(i, (i + by) % count) for i in range(count)])


def offsets_table():
    cell_count = TH * TW
    table = np.zeros((cell_count, cell_count, 9), np.float32)
    for source_cell in range(cell_count):
        for target_cell in range(cell_count):
            row_step = target_cell // TW - source_cell // TW
            col_step = target_cell % TW - source_cell % TW
            if abs(row_step) <= 1 and abs(col_step) <= 1:
                table[source_cell, target_cell, (row_step + 1) * 3 + col_step + 1] = 1.0
    return table


def by_group(rows, group_width):
    tile_count = rows.shape[0]
    cell_count = rows.shape[1]
    group_count = rows.shape[2] // group_width
    split = rows.reshape(tile_count, cell_count, group_count, group_width).transpose(2, 0, 1, 3)
    return split.reshape(group_count, tile_count, cell_count * group_width)


def transpose_conv(scaled_grads, weight):
    tile_count = scaled_grads.shape[0]
    cell_count = scaled_grads.shape[1]
    group_width = weight.shape[1]
    channels = weight.shape[2]
    group_count = channels // group_width
    selector = jnp.asarray(offsets_table(), jnp.bfloat16)
    split_weight = weight.reshape(9, group_width, group_count, group_width)
    blocks = jnp.einsum(
        "pqt,tcgo->gpoqc", selector, split_weight, preferred_element_type=jnp.float32
    )
    blocks = blocks.astype(jnp.bfloat16).reshape(
        group_count, cell_count * group_width, cell_count * group_width
    )
    grouped = by_group(scaled_grads, group_width)
    result = jnp.einsum("gnk,gkm->gnm", grouped, blocks, preferred_element_type=jnp.float32)
    result = result.reshape(group_count, tile_count, cell_count, group_width).transpose(1, 2, 0, 3)
    return result.reshape(tile_count, cell_count, channels)


def weight_corr(inputs, scaled_grads, group_width):
    cell_count = inputs.shape[1]
    channels = inputs.shape[2]
    group_count = channels // group_width
    grouped_inputs = by_group(inputs, group_width)
    grouped_grads = by_group(scaled_grads, group_width)
    moments = jnp.einsum(
        "gnk,gnm->gkm", grouped_inputs, grouped_grads, preferred_element_type=jnp.float32
    )
    moments = moments.reshape(group_count, cell_count, group_width, cell_count, group_width)
    selector = jnp.asarray(offsets_table(), jnp.float32)
    taps = jnp.einsum("gpcqo,qpt->tcgo", moments, selector, precision=lax.Precision.HIGHEST)
    return taps.reshape(9, group_width, channels)


def body(activations, upstream, routes, gate_codes, weights):
    incoming = shifted(upstream, "segment", -1)[0]
    inputs = activations[0]
    route_ids = routes[0]
    code_values = gate_codes[0].astype(jnp.float32)
    kernel = weights[0, 0]
    group_width = kernel.shape[1]
    per_device = inputs.shape[0]
    cell_count = inputs.shape[1]
    channels = inputs.shape[2]
    experts = lax.axis_size("expert")
    capacity = max(2, 4 * per_device // experts)
    gate_share = code_values / jnp.sum(code_values, axis=1, keepdims=True)
    scaled_grads = (gate_share[:, :, None, None] * incoming[:, None].astype(jnp.float32)).astype(
        jnp.bfloat16
    )
    grad_rows = scaled_grads.reshape(2 * per_device, cell_count * channels)
    input_rows = jnp.repeat(inputs, 2, axis=0).reshape(2 * per_device, cell_count * channels)
    flat_expert = route_ids.reshape(-1)
    matches = (flat_expert[:, None] == jnp.arange(experts, dtype=jnp.int32)[None, :]).astype(
        jnp.int32
    )
    earlier = jnp.cumsum(matches, axis=0) - matches
    slot_rank = jnp.sum(earlier * matches, axis=1)
    slot_place = flat_expert * capacity + slot_rank
    chooser = (
        slot_place[None, :] == jnp.arange(experts * capacity, dtype=jnp.int32)[:, None]
    ).astype(jnp.bfloat16)

    def pack_slots(rows):
        packed = jnp.dot(chooser, rows, preferred_element_type=jnp.float32).astype(jnp.bfloat16)
        return packed.reshape(experts, capacity, cell_count, channels)

    inputs_recv, grads_recv = (
        lax.all_to_all(pack_slots(input_rows), "expert", split_axis=0, concat_axis=0, tiled=True),
        lax.all_to_all(pack_slots(grad_rows), "expert", split_axis=0, concat_axis=0, tiled=True),
    )
    flat_grads = grads_recv.reshape(experts * capacity, cell_count, channels)
    answers = transpose_conv(flat_grads, kernel).astype(jnp.bfloat16)
    returned = lax.all_to_all(
        answers.reshape(experts, capacity, cell_count, channels),
        "expert",
        split_axis=0,
        concat_axis=0,
        tiled=True,
    )
    flat_inputs = inputs_recv.reshape(experts * capacity, cell_count, channels)
    local_grad = weight_corr(flat_inputs, flat_grads, group_width)
    flat_answers = returned.reshape(experts * capacity, cell_count * channels)
    per_route = jnp.dot(chooser.T, flat_answers, preferred_element_type=jnp.float32).reshape(
        per_device, 2, cell_count, channels
    )
    input_grad = (incoming.astype(jnp.float32) + per_route[:, 0] + per_route[:, 1]).astype(
        jnp.bfloat16
    )
    total_grad = lax.psum(local_grad, "dp") / per_device
    return (input_grad[None], total_grad[None, None])


LINE = 4
CORES = 2
NEAR_PAIRS = [(0, 1), (1, 0), (2, 3), (3, 2)]
SWAP = [(0, 1), (1, 0)]
VMEM_LIMIT = 16 * 1024 * 1024


def inner_pairs():
    crossing = {1: 2, 2: 1}
    pairs = []
    for e in range(LINE):
        for d in range(CORES):
            target = (crossing[e], d) if e in crossing else (e, 1 - d)
            pairs.append((CORES * e + d, CORES * target[0] + target[1]))
    return pairs


def fits_line(mesh):
    return mesh.shape["expert"] == LINE and mesh.shape["dp"] == CORES


def cell_order():
    return [row * TW + col for col in range(TW) for row in range(TH)]


def own_gates(info, expert):
    codes = info[2:4].astype(jnp.float32)
    hits = jnp.where(info[0:2] == expert, codes, 0.0)
    return (hits[0:1] + hits[1:2]) / (codes[0:1] + codes[1:2])


def gate_columns(info_ref, experts):
    rows = [own_gates(info_ref[...], expert) for expert in experts]
    count = rows[0].shape[1]
    table = jnp.concatenate(rows + [jnp.zeros((128 - len(rows), count), jnp.float32)], axis=0)
    table = jnp.concatenate([table, jnp.zeros((128, 128 - count), jnp.float32)], axis=1)
    return table.T[:count]


def slot_experts():
    me = lax.axis_index("expert")
    outer = (me == 0) | (me == 3)
    mid = jnp.where(outer, 2, 3)
    far = 5 - mid
    return [me, me ^ 1, me ^ mid, me ^ far]


def rows_by_cell(refs, wide):
    strips = refs[0].shape[1] // 128
    tiles = refs[0].shape[0] // (TH * TW)
    for at, ref in enumerate(refs):
        for strip in range(strips):
            wide[at * strips + strip] = ref[:, pl.ds(strip * 128, 128)].astype(jnp.float32)

    def cell_rows(at, cell):
        pieces = [wide[at * strips + strip, pl.ds(cell, tiles, stride=TH * TW), :] for strip in range(strips)]
        return jnp.concatenate(pieces, axis=1)

    return cell_rows


def turn_kernel(act_a, act_b, turned, wide, cells):
    width = act_a.shape[1]
    block = 2 * act_a.shape[0] // (TH * TW)
    column = TH * block
    cell_rows = rows_by_cell((act_a, act_b), wide)
    for place, cell in enumerate(cell_order()):
        act_rows = jnp.concatenate([cell_rows(0, cell), cell_rows(1, cell)], axis=0)
        cells[pl.ds(place * block, block), :] = act_rows.astype(jnp.bfloat16)
    empty = jnp.zeros((block, width), jnp.bfloat16)
    for col in range(TW):
        rows = cells[pl.ds(col * column, column), :]
        turned[1, :, pl.ds(col * column, column)] = rows.T
        turned[2, :, pl.ds(col * column, column)] = jnp.concatenate([rows[block:], empty], axis=0).T
        turned[0, :, pl.ds(col * column, column)] = jnp.concatenate([empty, rows[:-block]], axis=0).T


def prepare_kernel(grad_a, grad_b, turned, info_a, info_b, cells, gates, far_ref, wide, scaled):
    tiles = info_a.shape[1]
    block = 2 * tiles
    cell_rows = rows_by_cell((grad_a, grad_b), wide)
    experts = slot_experts()
    gates[pl.ds(0, tiles), :] = gate_columns(info_a, experts)
    gates[pl.ds(tiles, tiles), :] = gate_columns(info_b, experts)
    far_gate = gates[:, 3:4]
    for place, cell in enumerate(cell_order()):
        both = jnp.concatenate([cell_rows(0, cell), cell_rows(1, cell)], axis=0)
        cells[pl.ds(place * block, block), :] = both.astype(jnp.bfloat16)
        scaled[0, pl.ds(place * block, block), :] = (both * far_gate).astype(jnp.bfloat16)
    kernel_gradient(turned, scaled, 0, far_ref)


def kernel_gradient(turned, scaled_ref, slot, ref):
    width, column = turned.shape[1], turned.shape[2] // TW
    low_half = lax.broadcasted_iota(jnp.int32, (64, 128), 1) < 64
    for row_off in (-1, 0, 1):
        for col_off in (-1, 0, 1):
            lhs = turned[row_off + 1]
            rhs = scaled_ref[slot]
            if col_off == 1:
                lhs, rhs = lhs[:, column:], rhs[:column]
            if col_off == -1:
                lhs, rhs = lhs[:, :column], rhs[column:]
            full = jnp.dot(lhs, rhs, preferred_element_type=jnp.float32)
            tap = (row_off + 1) * 3 + col_off + 1
            for pair in range(width // 128):
                base = pair * 128
                piece = jnp.where(
                    low_half,
                    full[base : base + 64, base : base + 128],
                    full[base + 64 : base + 128, base : base + 128],
                )
                ref[tap, :, pl.ds(base, 128)] = piece.astype(ref.dtype)


def partial_kernel(cells, gates, turned, scaled_ref, mid_ref, near_ref, own_ref):
    block = gates.shape[0]
    for place in range(TH * TW):
        rows = cells[pl.ds(place * block, block), :].astype(jnp.float32)
        for slot in range(4):
            scaled_ref[slot, pl.ds(place * block, block), :] = (rows * gates[:, slot : slot + 1]).astype(jnp.bfloat16)
    for slot, ref in ((2, mid_ref), (1, near_ref), (0, own_ref)):
        kernel_gradient(turned, scaled_ref, slot, ref)


def add_answers(scaled_ref, slots, kernels, total):
    width = total.shape[1]
    block = total.shape[0] // (TH * TW)
    lane_group = lax.broadcasted_iota(jnp.int32, (64, width), 1) // 64
    masks = [jnp.where(lane_group == g, 1.0, 0.0).astype(jnp.bfloat16) for g in range(width // 64)]
    for slot, ref in zip(slots, kernels):
        for row_off in (-1, 0, 1):
            for col_off in (-1, 0, 1):
                tap = (row_off + 1) * 3 + col_off + 1
                kernel = ref[tap]
                blocks = jnp.concatenate([kernel * mask for mask in masks], axis=0)
                first = max(0, -row_off)
                rows = (TH - abs(row_off)) * block
                for col in range(TW):
                    if not 0 <= col + col_off < TW:
                        continue
                    source = (col * TH + first) * block
                    target = ((col + col_off) * TH + first + row_off) * block
                    total[pl.ds(target, rows), :] += lax.dot_general(
                        scaled_ref[slot, pl.ds(source, rows), :],
                        blocks,
                        (((1,), (1,)), ((), ())),
                        preferred_element_type=jnp.float32,
                    )


def early_answer_kernel(scaled_ref, own_ref, near_ref, mid_ref, total):
    total[...] = jnp.zeros_like(total)
    add_answers(scaled_ref, (0, 1, 2), (own_ref, near_ref, mid_ref), total)


def late_answer_kernel(scaled_ref, far_ref, early, grad_a, grad_b, out_a, out_b, total, spread):
    tiles = grad_a.shape[0] // (TH * TW)
    block = 2 * tiles
    strips = grad_a.shape[1] // 128
    total[...] = early[...]
    add_answers(scaled_ref, (3,), (far_ref,), total)
    for at, (grad, out) in enumerate(((grad_a, out_a), (grad_b, out_b))):
        for strip in range(strips):
            lanes = pl.ds(strip * 128, 128)
            for place, cell in enumerate(cell_order()):
                spread[strip, pl.ds(cell, tiles, stride=TH * TW), :] = total[
                    pl.ds(place * block + at * tiles, tiles), lanes
                ]
            out[:, lanes] = (grad[:, lanes].astype(jnp.float32) + spread[strip]).astype(jnp.bfloat16)


def place_half_kernel(scale, side, core_ref, half_ref, *refs):
    out, staged, done = refs[-3:]
    taps, _, width = half_ref.shape
    at = core_ref[0] if side == 0 else 1 - core_ref[0]
    lanes = pl.ds(pl.multiple_of(at * width, width), width)
    copies = []
    for tap in range(0, taps, 3):
        these = pl.ds(tap, min(3, taps - tap))
        staged[these] = half_ref[these].astype(jnp.float32) * scale
        copies.append(pltpu.make_async_copy(staged.at[these], out.at[these, :, lanes], done.at[tap]))
        copies[-1].start()
    for copy in copies:
        copy.wait()


def place_half(scale, side, core_at, half, begun=None):
    taps, group_width, width = half.shape
    specs = [pl.BlockSpec(memory_space=pltpu.SMEM)] + on_vmem(1)
    operands = [core_at, half]
    if begun is not None:
        specs.append(pl.BlockSpec(memory_space=pl.ANY))
        operands.append(begun)
    return pl.pallas_call(
        functools.partial(place_half_kernel, scale, side),
        out_shape=jax.ShapeDtypeStruct((taps, group_width, 2 * width), jnp.float32),
        in_specs=specs,
        out_specs=pl.BlockSpec(memory_space=pl.ANY),
        scratch_shapes=[
            pltpu.VMEM((taps, group_width, width), jnp.float32),
            pltpu.SemaphoreType.DMA((taps,)),
        ],
        input_output_aliases={} if begun is None else {2: 0},
        compiler_params=pltpu.CompilerParams(vmem_limit_bytes=VMEM_LIMIT),
        cost_estimate=pl.CostEstimate(flops=1000, bytes_accessed=1000, transcendentals=0),
    )(*operands)


def on_vmem(count):
    return [pl.BlockSpec(memory_space=pltpu.VMEM)] * count


def local_call(kernel, outs, scratch, flops, *operands):
    return pl.pallas_call(
        kernel,
        out_shape=tuple(outs),
        in_specs=on_vmem(len(operands)),
        out_specs=tuple(on_vmem(len(outs))),
        scratch_shapes=scratch,
        compiler_params=pltpu.CompilerParams(vmem_limit_bytes=VMEM_LIMIT),
        cost_estimate=pl.CostEstimate(flops=flops, bytes_accessed=1000, transcendentals=0),
    )(*operands)


def copy_kernel(source, out):
    out[...] = source[...]


def weights_travel(activations, upstream, routes, gate_codes, weights):
    me = lax.axis_index("expert")
    core = lax.axis_index("dp")
    inner = (me == 1) | (me == 2)
    per_device, cell_count, channels = activations.shape[1:]
    rows = per_device * cell_count
    width = channels // 2
    taps, group_width = weights.shape[2:4]
    sections = lax.axis_size("segment")

    def half(array, which):
        return lax.dynamic_slice_in_dim(array, which * width, width, array.ndim - 1)

    def near(array):
        return lax.ppermute(array, "expert", NEAR_PAIRS)

    def across(array):
        return lax.ppermute(array, ("expert", "dp"), inner_pairs())

    def from_next(array):
        return lax.ppermute(array, "segment", [((s + 1) % sections, s) for s in range(sections)])

    info = jnp.concatenate([routes[0].T, gate_codes[0].T], axis=0)
    info_b = lax.ppermute(info, "dp", SWAP)
    grad_rows = from_next(upstream[0].reshape(rows, channels))
    my_weights = half(weights[0, 0], core)
    inner_weights = across(my_weights)
    (inner_weights,) = local_call(
        copy_kernel,
        (jax.ShapeDtypeStruct(inner_weights.shape, inner_weights.dtype),),
        [],
        8_000_000_000,
        inner_weights,
    )
    act_rows = activations[0].reshape(rows, channels)
    act_a = half(act_rows, core)
    act_b = lax.ppermute(half(act_rows, 1 - core), "dp", SWAP)
    near_weights = near(my_weights)
    grad_a = half(grad_rows, core)
    grad_b = lax.ppermute(half(grad_rows, 1 - core), "dp", SWAP)

    part = jax.ShapeDtypeStruct((taps, group_width, width), jnp.bfloat16)
    (turned,) = local_call(
        turn_kernel,
        (jax.ShapeDtypeStruct((3, width, 2 * rows), jnp.bfloat16),),
        [
            pltpu.VMEM((2 * (width // 128), rows, 128), jnp.float32),
            pltpu.VMEM((2 * rows, width), jnp.bfloat16),
        ],
        200_000_000,
        act_a, act_b,
    )
    cells, gates, far_part = local_call(
        prepare_kernel,
        (
            jax.ShapeDtypeStruct((2 * rows, width), jnp.bfloat16),
            jax.ShapeDtypeStruct((2 * per_device, 128), jnp.float32),
            part,
        ),
        [
            pltpu.VMEM((2 * (width // 128), rows, 128), jnp.float32),
            pltpu.VMEM((1, 2 * rows, width), jnp.bfloat16),
        ],
        600_000_000,
        grad_a, grad_b, turned, info, info_b,
    )
    cross_weights = across(near_weights)
    first_swap = near(jnp.where(inner, inner_weights, far_part))
    scaled, mid_part, near_part, own_part = local_call(
        partial_kernel,
        (
            jax.ShapeDtypeStruct((4, 2 * rows, width), jnp.bfloat16),
            part,
            part,
            jax.ShapeDtypeStruct((taps, group_width, width), jnp.float32),
        ),
        [],
        1_200_000_000,
        cells, gates, turned,
    )
    first_swap, mid_part = lax.optimization_barrier((first_swap, mid_part))
    second_swap = near(jnp.where(inner, cross_weights, mid_part))
    far_sum = across(far_part + first_swap)
    mid_sum = across(mid_part + second_swap)
    last_swap = near(jnp.where(inner, near_part + far_sum, near_part))

    mid_weights = jnp.where(inner, inner_weights, first_swap)
    far_weights = jnp.where(inner, cross_weights, second_swap)
    (early,) = local_call(
        early_answer_kernel,
        (jax.ShapeDtypeStruct((2 * rows, width), jnp.float32),),
        [],
        1_200_000_000,
        scaled, my_weights, near_weights, mid_weights,
    )
    answer = jax.ShapeDtypeStruct((rows, width), jnp.bfloat16)
    grad_own, grad_other = local_call(
        late_answer_kernel,
        (answer, answer),
        [
            pltpu.VMEM((2 * rows, width), jnp.float32),
            pltpu.VMEM((width // 128, rows, 128), jnp.float32),
        ],
        500_000_000,
        scaled, far_weights, early, grad_a, grad_b,
    )
    grad_back = lax.ppermute(grad_other, "dp", SWAP)

    def whole(mine, other):
        return jnp.where(
            core == 0, jnp.concatenate([mine, other], axis=-1), jnp.concatenate([other, mine], axis=-1)
        )

    input_grad = whole(grad_own, grad_back).reshape(per_device, cell_count, channels)
    last_swap, input_grad = lax.optimization_barrier((last_swap, input_grad))
    kernel_sum = own_part + last_swap.astype(jnp.float32) + jnp.where(inner, mid_sum, 0).astype(jnp.float32)
    kernel_mine = kernel_sum.astype(jnp.bfloat16)
    kernel_other = lax.ppermute(kernel_mine, "dp", SWAP)
    core_at = jnp.reshape(core, (1,)).astype(jnp.int32)
    begun = place_half(1.0 / per_device, 0, core_at, kernel_mine)
    weight_grad = place_half(1.0 / per_device, 1, core_at, kernel_other, begun)
    return (input_grad[None], weight_grad[None, None])


def solution(mesh):
    placed = (
        P("segment", ("expert", "dp"), None, None),
        P("segment", ("expert", "dp"), None, None),
        P("segment", ("expert", "dp"), None),
        P("segment", ("expert", "dp"), None),
        P("segment", "expert", None, None, None),
    )
    step = weights_travel if fits_line(mesh) else body
    return jax.shard_map(
        step,
        mesh=mesh,
        in_specs=placed,
        out_specs=(
            P("segment", ("expert", "dp"), None, None),
            P("segment", "expert", None, None, None),
        ),
        check_vma=False,
    )
```
